256 devices in a mesh: slab: 2 (over z_hi), row: 8 (over x, core), col: 16 (over y, z_lo).
Axes of the slice: x: 4, y: 4, z: 8 (z_hi: 2, z_lo: 4; z = z_hi * 4 + z_lo), core: 2. Of those that a mesh axis runs over, the one named last changes fastest.
Arguments:
- pair_act: bfloat16 [512, 512, 128], P('row', 'col'), may hold values from -6 to 6
- out_grad: bfloat16 [512, 512, 128], P('row', 'col'), may hold values from -6 to 6
- pair_mask: int32 [512, 512], P('row', 'col'), may hold values 0 or 1
- chain_starts: int32 [6], replicated, may hold values from 0 to 511, as said below
- in_gain: float32 [128], replicated, may hold values from 0.25 to 1.75
- in_bias: float32 [128], replicated, may hold values from -3 to 3
- w_proj: bfloat16 [128, 512], replicated, may hold values from -0.5 to 0.5
- w_gate: bfloat16 [128, 128], replicated, may hold values from -0.5 to 0.5
- w_out: bfloat16 [128, 128], replicated, may hold values from -0.5 to 0.5
- mid_gain: float32 [128], replicated, may hold values from 0.25 to 1.75
- mid_bias: float32 [128], replicated, may hold values from -3 to 3
Outputs:
- pair_grad: bfloat16 [512, 16, 2, 16, 128], P('row', 'col', 'slab')
The draws below stay inside these ranges and needn't reach their ends.
Inputs may be any that keep to these rules, and one draw needn't show every extreme that they name: `chain_starts`: rising, distinct, the first entry 0 and the last entry 511.
All inputs are finite; a program needn't handle non-finite values. No bound on the sum of `pair_mask` on one device may be relied on, other than what follows from the above.
Results may differ from the reference program's by a relative error of at most 0.022.
Values may be sent and summed in bfloat16 or wider, within the bound.
No kernel may reach another device: no remote copies, remote signals or barrier semaphores. Data moves between devices by JAX's collectives and lax.ppermute only.
A program may use at most 128 MiB of HBM per device.

```python
import jax
import jax.numpy as jnp
from jax import lax

PAIR = 128
HIDDEN_SIZE = 128
RESIDUES = 512
CHAINS = 6
N_SLAB = 2
N_COL = 16


def draw_chain_starts(key, part):
    key = jax.random.fold_in(key, 7)
    picked = jax.random.permutation(key, RESIDUES - 2)[:CHAINS - 2] + 1
    inner = jnp.sort(picked).astype(jnp.int32)
    return jnp.concatenate([jnp.zeros((1,), jnp.int32), inner, jnp.full((1,), RESIDUES - 1, jnp.int32)])


def with_ends(drawn, own_key, low, high):
    place = [jax.random.randint(jax.random.fold_in(own_key, axis), (), 0, length) for axis, length in enumerate(drawn.shape)]
    longest = drawn.shape.index(max(drawn.shape))
    neighbour = place[:longest] + [(place[longest] + 1) % drawn.shape[longest]] + place[longest + 1:]
    return drawn.at[tuple(place)].set(low).at[tuple(neighbour)].set(high)


def shard_levels(own_key, dims, cuts, least, high):
    def one(dim, blocks):
        draws = jax.random.uniform(jax.random.fold_in(jax.random.fold_in(own_key, 6), dim), (blocks,), jnp.float32, least / len(cuts), high / len(cuts))
        return jnp.repeat(jnp.exp(draws), dims[dim] // blocks).reshape((-1,) + (1,) * (len(dims) - dim - 1))

    gain = one(*cuts[0])
    for cut in cuts[1:]:
        gain = gain * one(*cut)
    return gain


def noise(own_key, shape, width, limit, pieces=(), kind=jnp.bfloat16):
    values = width * jax.random.normal(own_key, shape, jnp.float32)
    if pieces:
        values = values * shard_levels(own_key, shape, pieces, -0.22, 0.18)
    return jnp.clip(values, -limit, limit).astype(kind)


def setup_inputs(seed: int = 0) -> dict:
    splits = jax.random.split(jax.random.key(seed), 12)
    return {
        "pair_act": noise(splits[0], (RESIDUES, RESIDUES, PAIR), 1.0, 6.0, ((0, 8), (1, 16))),
        "out_grad": noise(splits[1], (RESIDUES, RESIDUES, PAIR), 1.0, 6.0, ((0, 8), (1, 16))),
        "pair_mask": with_ends((jax.random.randint(splits[2], (RESIDUES, RESIDUES), 0, 4) < 3).astype(jnp.int32), jax.random.fold_in(splits[2], 1), 0, 1),
        "chain_starts": draw_chain_starts(jax.random.fold_in(splits[11], 71), 0),
        "in_gain": jnp.clip(1.0 + 0.15 * jax.random.normal(splits[4], (PAIR,), jnp.float32), 0.25, 1.75),
        "in_bias": noise(splits[5], (PAIR,), 0.5, 3.0, (), jnp.float32),
        "w_proj": noise(splits[6], (PAIR, 4 * HIDDEN_SIZE), PAIR ** -0.5, 0.5),
        "w_gate": noise(splits[7], (PAIR, PAIR), PAIR ** -0.5, 0.5),
        "w_out": noise(splits[8], (HIDDEN_SIZE, PAIR), HIDDEN_SIZE ** -0.5, 0.5),
        "mid_gain": jnp.clip(1.0 + 0.15 * jax.random.normal(splits[9], (HIDDEN_SIZE,), jnp.float32), 0.25, 1.75),
        "mid_bias": noise(splits[10], (HIDDEN_SIZE,), 0.5, 3.0, (), jnp.float32),
    }


def normalize(values):
    average = lax.optimization_barrier(jnp.mean(values, axis=-1, keepdims=True))
    centred = values - average
    inv_std = lax.rsqrt(lax.optimization_barrier(jnp.mean(centred * centred, axis=-1, keepdims=True)) + 1e-05)
    return (centred * inv_std, inv_std)

def norm_backward(grad_normed, normed, inv_std):
    first = lax.optimization_barrier(jnp.mean(grad_normed, axis=-1, keepdims=True))
    second = lax.optimization_barrier(jnp.mean(grad_normed * normed, axis=-1, keepdims=True))
    return (grad_normed - first - normed * second) * inv_std

def chain_keep(pair_mask, chain_starts, row_ids, col_ids):
    row_chain = lax.optimization_barrier(jnp.sum((row_ids[:, None] >= chain_starts[None, :]).astype(jnp.int32), axis=1))
    col_chain = lax.optimization_barrier(jnp.sum((col_ids[:, None] >= chain_starts[None, :]).astype(jnp.int32), axis=1))
    same_chain = row_chain[:, None] == col_chain[None, :]
    return jnp.where(same_chain | (pair_mask > 0), 1.0, 0.0).astype(jnp.float32)

def gated_pair(projected, keep_mask):
    left_gate, left_val, right_gate, right_val = jnp.split(projected, 4, axis=-1)
    keep_wide = keep_mask[..., None]
    left = (keep_wide * jax.nn.sigmoid(left_gate) * left_val).astype(jnp.bfloat16)
    right = (keep_wide * jax.nn.sigmoid(right_gate) * right_val).astype(jnp.bfloat16)
    return (left, right)

def gating_backward(left_grad, right_grad, projected, keep_mask):
    left_gate, left_val, right_gate, right_val = jnp.split(projected, 4, axis=-1)
    sig_left = jax.nn.sigmoid(left_gate)
    sig_right = jax.nn.sigmoid(right_gate)
    keep_wide = keep_mask[..., None]
    parts = [left_grad * keep_wide * left_val * sig_left * (1.0 - sig_left), left_grad * keep_wide * sig_left, right_grad * keep_wide * right_val * sig_right * (1.0 - sig_right), right_grad * keep_wide * sig_right]
    return jnp.concatenate(parts, axis=-1).astype(jnp.bfloat16)

def flat_dot(values, matrix):
    lead = values.shape[:-1]
    flat = values.reshape(-1, values.shape[-1])
    return jnp.dot(flat, matrix, preferred_element_type=jnp.float32).reshape(lead + (matrix.shape[1],))

def reference(pair_act, out_grad, pair_mask, chain_starts, in_gain, in_bias, w_proj, w_gate, w_out, mid_gain, mid_bias):
    normed, inv_std = normalize(pair_act.astype(jnp.float32))
    x_in = (normed * in_gain + in_bias).astype(jnp.bfloat16)
    residue = jnp.arange(RESIDUES, dtype=jnp.int32)
    keep_mask = chain_keep(pair_mask, chain_starts, residue, residue)
    projected = flat_dot(x_in, w_proj)
    left, right = gated_pair(projected, keep_mask)
    left_f = left.astype(jnp.float32)
    right_f = right.astype(jnp.float32)
    triangle = jnp.einsum('ikc,jkc->ijc', left_f, right_f, precision=lax.Precision.HIGHEST)
    tri_hat, tri_inv = normalize(triangle)
    mid_out = (tri_hat * mid_gain + mid_bias).astype(jnp.bfloat16)
    gate = jax.nn.sigmoid(flat_dot(x_in, w_gate))
    proj_out = flat_dot(mid_out, w_out)
    grad_in = out_grad.astype(jnp.float32)
    gate_grad = (grad_in * proj_out * gate * (1.0 - gate)).astype(jnp.bfloat16)
    mid_in_grad = (grad_in * gate).astype(jnp.bfloat16)
    grad_hat = flat_dot(mid_in_grad, w_out.T) * mid_gain
    tri_grad = norm_backward(grad_hat, tri_hat, tri_inv).astype(jnp.bfloat16)
    tri_grad_f = tri_grad.astype(jnp.float32)
    left_grad = jnp.einsum('ijc,jkc->ikc', tri_grad_f, right_f, precision=lax.Precision.HIGHEST)
    right_grad = jnp.einsum('ijc,ikc->jkc', tri_grad_f, left_f, precision=lax.Precision.HIGHEST)
    proj_grad = gating_backward(left_grad, right_grad, projected, keep_mask)
    x_grad = flat_dot(proj_grad, w_proj.T) + flat_dot(gate_grad, w_gate.T)
    result = norm_backward(x_grad * in_gain, normed, inv_std).astype(jnp.bfloat16)
    return result.reshape(RESIDUES, N_COL, N_SLAB, RESIDUES // (N_COL * N_SLAB), PAIR)
```

```python
import jax
import jax.numpy as jnp
from jax import lax
from jax.experimental import pallas as pl
from jax.experimental.pallas import tpu as pltpu
from jax.sharding import PartitionSpec as P

BF16 = jnp.bfloat16
F32 = jnp.float32
LANES = 128
ROWS = 64
HALF = 16
LOW = 8
CHANNELS = 128
POINTS = ROWS * HALF
PEERS = ("row", "col")
EVERYONE = ("row", "col", "slab")


def dot(a, b, ca, cb):
    return lax.dot_general(a, b, (((ca,), (cb,)), ((), ())), preferred_element_type=F32)


def place(k):
    return ((k % LOW) * (HALF // LOW) + k // LOW) * ROWS


def normalize(values):
    average = jnp.mean(values, axis=-1, keepdims=True)
    centred = values - average
    inv_std = lax.rsqrt(jnp.mean(centred * centred, axis=-1, keepdims=True) + 1e-05)
    return centred * inv_std, inv_std


def low_lanes(shape):
    return lax.broadcasted_iota(jnp.int32, shape, 1) < ROWS


def mix(a, b):
    low = low_lanes(a.shape)
    first = jnp.where(low, a, pltpu.roll(b, ROWS, 1))
    second = jnp.where(low, pltpu.roll(a, ROWS, 1), b)
    return first, second


def load_half(ref, slab_at, scratch):
    start = pl.multiple_of(slab_at * HALF, HALF)
    scratch[...] = ref[:, pl.ds(start, HALF), :].astype(F32).reshape(POINTS, LANES)


def column(scratch, k):
    return scratch[pl.ds(k, ROWS, stride=HALF), :]


def keep_rows(mask_ref, starts_ref, mask_t, slab_at, row_at, col_at):
    mask = mask_ref[...].astype(F32)
    twice = jnp.concatenate([mask, mask], axis=0)
    wide = jnp.concatenate([twice, jnp.zeros((LANES, LANES - mask.shape[1]), F32)], axis=1)
    mask_t[...] = wide.T
    start = pl.multiple_of(slab_at * HALF, HALF)
    own = mask_t[pl.ds(start, HALF), :]
    shape = (HALF, LANES)
    lane = lax.broadcasted_iota(jnp.int32, shape, 1)
    row_ids = row_at * ROWS + jnp.where(lane < ROWS, lane, lane - ROWS)
    col_ids = (col_at * 2 + slab_at) * HALF + lax.broadcasted_iota(jnp.int32, shape, 0)
    row_chain = jnp.zeros(shape, jnp.int32)
    col_chain = jnp.zeros(shape, jnp.int32)
    for at in range(starts_ref.shape[0]):
        start_at = starts_ref[at]
        row_chain = row_chain + (row_ids >= start_at).astype(jnp.int32)
        col_chain = col_chain + (col_ids >= start_at).astype(jnp.int32)
    return jnp.where((row_chain == col_chain) | (own > 0.0), 1.0, 0.0)


def edges_kernel(
    starts_ref, act_ref, mask_ref, gain_ref, bias_ref, w_ref, edges_ref, x_ref, keep_ref, tile, mask_t, projected, turned
):
    slab_at = lax.axis_index("slab")
    load_half(act_ref, slab_at, tile)
    keep_ref[...] = keep_rows(
        mask_ref, starts_ref, mask_t, slab_at, lax.axis_index("row"), lax.axis_index("col")
    )
    for k in range(HALF):
        normed, _ = normalize(column(tile, k))
        x_ref[pl.ds(place(k), ROWS), :] = (normed * gain_ref[...] + bias_ref[...]).astype(BF16)
    projected[...] = dot(x_ref[...], w_ref[...], 1, 0)
    for k in range(HALF):
        here = pl.ds(place(k), ROWS)
        left = jax.nn.sigmoid(projected[here, 0:128]) * projected[here, 128:256]
        right = jax.nn.sigmoid(projected[here, 256:384]) * projected[here, 384:512]
        both = jnp.concatenate([left, right], axis=0).T
        turned[pl.ds(k, CHANNELS, stride=HALF), :] = both * keep_ref[k : k + 1, :]
    edges_ref[...] = turned[...].astype(BF16)


def triangle_kernel(edges_ref, out_ref, left_ref, right_ref):
    depth = edges_ref.shape[0] // 8
    for m in range(4):
        a = edges_ref[pl.ds(2 * m * depth, depth), :].astype(F32)
        b = edges_ref[pl.ds((2 * m + 1) * depth, depth), :].astype(F32)
        left, right = mix(a, b)
        left_ref[:, m * LANES : (m + 1) * LANES] = left.astype(BF16)
        right_ref[:, m * LANES : (m + 1) * LANES] = right.astype(BF16)
    for m in range(4):
        tri = dot(right_ref[...], left_ref[:, m * LANES : (m + 1) * LANES], 0, 0)
        tri = tri.reshape(32, HALF, LANES)
        a = tri[:, 0:LOW, :].reshape(depth, LANES)
        b = tri[:, LOW:HALF, :].reshape(depth, LANES)
        first, second = mix(a, b)
        out_ref[pl.ds(2 * m * depth, depth), :] = first.astype(BF16)
        out_ref[pl.ds((2 * m + 1) * depth, depth), :] = second.astype(BF16)


def middle_kernel(
    tri_ref, grad_ref, x_ref, w_gate_ref, w_out_ref, gain_ref, bias_ref, out_ref, gate_grad_ref, tile, hats, turned
):
    slab_at = lax.axis_index("slab")
    load_half(grad_ref, slab_at, tile)
    parts = tri_ref[...].astype(F32).reshape(CHANNELS, HALF, LANES)
    tri = parts[:, 0:LOW, :] + parts[:, LOW:HALF, :]
    average = jnp.mean(tri, axis=0, keepdims=True)
    centred = tri - average
    inv = lax.rsqrt(jnp.mean(centred * centred, axis=0, keepdims=True) + 1e-05)
    hats[...] = (centred * inv).reshape(CHANNELS * LOW, LANES)
    gain = jnp.broadcast_to(gain_ref[...], (CHANNELS, LANES)).T
    bias = jnp.broadcast_to(bias_ref[...], (CHANNELS, LANES)).T
    for low in range(LOW):
        here = pl.ds(low * LANES, LANES)
        hat = hats[pl.ds(low, CHANNELS, stride=LOW), :]
        mid_out = (hat * gain + bias).astype(BF16)
        proj_out = dot(mid_out, w_out_ref[...], 0, 0)
        gate = jax.nn.sigmoid(dot(x_ref[here, :], w_gate_ref[...], 1, 0))
        grad_in = jnp.concatenate([column(tile, low), column(tile, low + LOW)], axis=0)
        gate_grad_ref[here, :] = (grad_in * proj_out * gate * (1.0 - gate)).astype(BF16)
        mid_in_grad = (grad_in * gate).astype(BF16)
        grad_hat = dot(w_out_ref[...], mid_in_grad, 1, 1) * gain
        first = jnp.mean(grad_hat, axis=0, keepdims=True)
        second = jnp.mean(grad_hat * hat, axis=0, keepdims=True)
        tri_grad = (grad_hat - first - hat * second) * inv[0, low : low + 1, :]
        turned[pl.ds(low, CHANNELS, stride=LOW), :] = tri_grad
    once = turned[...].reshape(CHANNELS, LOW, LANES)
    out_ref[...] = jnp.concatenate([once, once], axis=1).astype(BF16).reshape(CHANNELS * HALF, LANES)


def grads_kernel(tri_grad_ref, left_ref, right_ref, out_ref, grid_t):
    depth = tri_grad_ref.shape[0] // 8
    for m in range(4):
        a = tri_grad_ref[pl.ds(2 * m * depth, depth), :].astype(F32)
        b = tri_grad_ref[pl.ds((2 * m + 1) * depth, depth), :].astype(F32)
        first, second = mix(a, b)
        both = jnp.concatenate(
            [first.reshape(32, LOW, LANES), second.reshape(32, LOW, LANES)], axis=1
        )
        grid_t[:, m * LANES : (m + 1) * LANES] = both.reshape(32 * HALF, LANES).astype(BF16)
    for m in range(4):
        at = slice(m * LANES, (m + 1) * LANES)
        left_grad = dot(right_ref[...], grid_t[:, at], 1, 0)
        right_grad = dot(left_ref[...], grid_t[at, :], 1, 1)
        first, second = mix(left_grad, right_grad)
        out_ref[pl.ds(2 * m * depth, depth), :] = first.astype(BF16)
        out_ref[pl.ds((2 * m + 1) * depth, depth), :] = second.astype(BF16)


def final_kernel(
    grads_ref, act_ref, x_ref, keep_ref, gate_grad_ref, w_proj_ref, w_gate_ref, gain_ref, out_ref,
    tile, grads, projected, proj_grad, x_grad, result,
):
    slab_at = lax.axis_index("slab")
    load_half(act_ref, slab_at, tile)
    grads[...] = grads_ref[...].astype(F32)
    projected[...] = dot(x_ref[...], w_proj_ref[...], 1, 0)
    for k in range(HALF):
        here = pl.ds(place(k), ROWS)
        both = (grads[pl.ds(k, CHANNELS, stride=HALF), :] * keep_ref[k : k + 1, :]).T
        for side in range(2):
            grad = both[side * ROWS : (side + 1) * ROWS, :]
            at = side * 256
            sig = jax.nn.sigmoid(projected[here, at : at + 128])
            value = projected[here, at + 128 : at + 256]
            proj_grad[here, at : at + 128] = (grad * value * sig * (1.0 - sig)).astype(BF16)
            proj_grad[here, at + 128 : at + 256] = (grad * sig).astype(BF16)
    x_grad[...] = dot(proj_grad[...], w_proj_ref[...], 1, 1) + dot(gate_grad_ref[...], w_gate_ref[...], 1, 1)
    for k in range(HALF):
        normed, inv_std = normalize(column(tile, k))
        in_hat = x_grad[pl.ds(place(k), ROWS), :] * gain_ref[...]
        first = jnp.mean(in_hat, axis=-1, keepdims=True)
        second = jnp.mean(in_hat * normed, axis=-1, keepdims=True)
        result[pl.ds(k, ROWS, stride=HALF), :] = (in_hat - first - normed * second) * inv_std
    out_ref[...] = result[...].reshape(ROWS, HALF, LANES).astype(BF16)


SMEM = pl.BlockSpec(memory_space=pltpu.SMEM)
VMEM = pl.BlockSpec(memory_space=pltpu.VMEM)


def call(kernel, outs, scratch, args, name, smem=0):
    single = not isinstance(outs, list)
    return pl.pallas_call(
        kernel,
        out_shape=outs,
        in_specs=[SMEM] * smem + [VMEM] * (len(args) - smem),
        out_specs=VMEM if single else [VMEM] * len(outs),
        scratch_shapes=scratch,
        compiler_params=pltpu.CompilerParams(vmem_limit_bytes=24 * 1024 * 1024),
        name=name,
    )(*args)


def shape(dims, kind):
    return jax.ShapeDtypeStruct(dims, kind)


def exchange(flat, axes, pieces):
    cut = flat.reshape(pieces, flat.shape[0] // pieces, LANES)
    return lax.all_to_all(cut, axes, 0, 0, tiled=True).reshape(flat.shape)


def on_device(
    pair_act, out_grad, pair_mask, chain_starts, in_gain, in_bias, w_proj, w_gate, w_out, mid_gain, mid_bias
):
    in_gain, in_bias, mid_gain, mid_bias = (
        v.reshape(1, LANES) for v in (in_gain, in_bias, mid_gain, mid_bias)
    )
    peers = lax.axis_size("row") * lax.axis_size("col")
    rows = CHANNELS * HALF
    edges, x_in, keep = call(
        edges_kernel,
        [shape((rows, LANES), BF16), shape((POINTS, LANES), BF16), shape((HALF, LANES), F32)],
        [
            pltpu.VMEM((POINTS, LANES), F32),
            pltpu.VMEM((LANES, LANES), F32),
            pltpu.VMEM((POINTS, 512), F32),
            pltpu.VMEM((rows, LANES), F32),
        ],
        (chain_starts, pair_act, pair_mask, in_gain, in_bias, w_proj),
        "edges",
        smem=1,
    )
    edges = exchange(edges, PEERS, peers)
    tri, left, right = call(
        triangle_kernel,
        [shape((rows, LANES), BF16), shape((256, 512), BF16), shape((256, 512), BF16)],
        [],
        (edges,),
        "triangle",
    )
    tri = exchange(tri, EVERYONE, peers * 2)
    tri_grad, gate_grad = call(
        middle_kernel,
        [shape((rows, LANES), BF16), shape((POINTS, LANES), BF16)],
        [
            pltpu.VMEM((POINTS, LANES), F32),
            pltpu.VMEM((CHANNELS * LOW, LANES), F32),
            pltpu.VMEM((CHANNELS * LOW, LANES), F32),
        ],
        (tri, out_grad, x_in, w_gate, w_out, mid_gain, mid_bias),
        "middle",
    )
    tri_grad = exchange(tri_grad, EVERYONE, peers * 2)
    grads = call(
        grads_kernel,
        shape((rows, LANES), BF16),
        [pltpu.VMEM((512, 512), BF16)],
        (tri_grad, left, right),
        "grads",
    )
    grads = exchange(grads, PEERS, peers)
    result = call(
        final_kernel,
        shape((ROWS, HALF, LANES), BF16),
        [
            pltpu.VMEM((POINTS, LANES), F32),
            pltpu.VMEM((rows, LANES), F32),
            pltpu.VMEM((POINTS, 512), F32),
            pltpu.VMEM((POINTS, 512), BF16),
            pltpu.VMEM((POINTS, LANES), F32),
            pltpu.VMEM((POINTS, LANES), F32),
        ],
        (grads, pair_act, x_in, keep, gate_grad, w_proj, w_gate, in_gain),
        "final",
    )
    return result.reshape(ROWS, 1, 1, HALF, LANES)


def solution(mesh):
    in_specs = (
        P("row", "col", None),
        P("row", "col", None),
        P("row", "col"),
        P(),
        P(),
        P(),
        P(),
        P(),
        P(),
        P(),
        P(),
    )
    out_specs = P("row", "col", "slab", None, None)
    return jax.shard_map(
        on_device, mesh=mesh, in_specs=in_specs, out_specs=out_specs, check_vma=False
    )
```

```python
import jax
import jax.numpy as jnp
from jax import lax
from jax.experimental import pallas as pl
from jax.experimental.pallas import tpu as pltpu
from jax.sharding import Mesh
from jax.sharding import PartitionSpec as P

BF16 = jnp.bfloat16
F32 = jnp.float32
LANES = 128
ROWS = 64
HALF = 16
COLS = 2 * HALF
LOW = 8
CHANNELS = 128
OWN = CHANNELS // 2
POINTS = ROWS * HALF
LINES = 4
NEAR = ("x", "y", "z")
FAR = ("x", "y", "z", "slab")


def dot(a, b, ca, cb):
    return lax.dot_general(a, b, (((ca,), (cb,)), ((), ())), preferred_element_type=F32)


def place(k):
    return (k // HALF) * POINTS + ((k % LOW) * (HALF // LOW) + k % HALF // LOW) * ROWS


def normalize(values):
    average = jnp.mean(values, axis=-1, keepdims=True)
    centred = values - average
    inv_std = lax.rsqrt(jnp.mean(centred * centred, axis=-1, keepdims=True) + 1e-05)
    return centred * inv_std, inv_std


def mix(a, b):
    low = lax.broadcasted_iota(jnp.int32, a.shape, 1) < ROWS
    first = jnp.where(low, a, pltpu.roll(b, ROWS, 1))
    second = jnp.where(low, pltpu.roll(a, ROWS, 1), b)
    return first, second


def block(m):
    return slice(m * LANES, (m + 1) * LANES)


def load_half(ref, slab_at, scratch):
    start = pl.multiple_of(slab_at * HALF, HALF)
    scratch[...] = ref[:, pl.ds(start, HALF), :].astype(F32).reshape(POINTS, LANES)


def column(scratch, k, width=HALF):
    return scratch[pl.ds(k, ROWS, stride=width), :]


def keep_rows(mask_ref, starts_ref, slab_at, row_at, col_at):
    mask = mask_ref[...].astype(F32)
    twice = jnp.concatenate([mask, mask], axis=0)
    wide = jnp.concatenate([twice, jnp.zeros((LANES, LANES - COLS), F32)], axis=1)
    shape = (COLS, LANES)
    lane = lax.broadcasted_iota(jnp.int32, shape, 1)
    row_ids = row_at * ROWS + jnp.where(lane < ROWS, lane, lane - ROWS)
    col_ids = col_at * COLS + lax.broadcasted_iota(jnp.int32, shape, 0)
    row_chain = jnp.zeros(shape, jnp.int32)
    col_chain = jnp.zeros(shape, jnp.int32)
    for at in range(starts_ref.shape[0]):
        start_at = starts_ref[at]
        row_chain = row_chain + (row_ids >= start_at).astype(jnp.int32)
        col_chain = col_chain + (col_ids >= start_at).astype(jnp.int32)
    return jnp.where((row_chain == col_chain) | (wide.T[0:COLS, :] > 0.0), 1.0, 0.0)


def edges_kernel(
    starts_ref, act_ref, mask_ref, gain_ref, bias_ref, w_ref, edges_ref, x_ref, keep_ref, tile, kept, x_all, projected, turned
):
    slab_at = lax.axis_index("slab")
    row_at = lax.axis_index("x") * 2 + lax.axis_index("core")
    col_at = lax.axis_index("y") * 4 + lax.axis_index("z")
    tile[...] = act_ref[...].astype(F32).reshape(ROWS * COLS, LANES)
    kept[...] = keep_rows(mask_ref, starts_ref, slab_at, row_at, col_at)
    keep_ref[...] = kept[pl.ds(pl.multiple_of(slab_at * HALF, HALF), HALF), :]
    for k in range(COLS):
        normed, _ = normalize(column(tile, k, COLS))
        x_all[pl.ds(place(k), ROWS), :] = (normed * gain_ref[...] + bias_ref[...]).astype(BF16)
    x_ref[...] = x_all[pl.ds(pl.multiple_of(slab_at * POINTS, POINTS), POINTS), :]
    own = []
    for at in range(2):
        first, second = mix(w_ref[:, block(at)].astype(F32), w_ref[:, block(at + 2)].astype(F32))
        own.append(jnp.where(slab_at == 0, first, second).astype(BF16))
    projected[...] = dot(x_all[...], jnp.concatenate(own, axis=1), 1, 0)
    for k in range(HALF):
        parts = []
        for at in (k, k + HALF):
            here = pl.ds(place(at), ROWS)
            parts.append(jax.nn.sigmoid(projected[here, 0:128]) * projected[here, 128:256])
        both = jnp.concatenate(parts, axis=0).T
        low = lax.broadcasted_iota(jnp.int32, (1, LANES), 1) < ROWS
        both = both * jnp.where(low, kept[k : k + 1, :], kept[k + HALF : k + HALF + 1, :])
        turned[pl.ds(k, OWN, stride=COLS), :] = both[0:OWN, :]
        turned[pl.ds(k + HALF, OWN, stride=COLS), :] = both[OWN:CHANNELS, :]
    edges_ref[...] = turned[...].astype(BF16)


def sort_kernel(edges_ref, left_ref, right_ref):
    for m in range(LINES // 2):
        pair = edges_ref[pl.ds(m * 1024, 1024), :].astype(F32).reshape(2, 16, COLS, LANES)
        for side, ref in enumerate((left_ref, right_ref)):
            a, b = (
                pair[at, :, side * HALF : (side + 1) * HALF, :].reshape(16 * HALF, LANES)
                for at in range(2)
            )
            first, second = mix(a, b)
            both = jnp.concatenate(
                [first.reshape(16, HALF, LANES), second.reshape(16, HALF, LANES)], axis=1
            )
            ref[:, block(m)] = both.reshape(512, LANES).astype(BF16)


def triangle_kernel(left_ref, own_ref, other_ref, out_ref, right_ref):
    core_at = lax.axis_index("core")
    for m in range(LINES // 2):
        own, other = own_ref[:, block(m)].astype(F32), other_ref[:, block(m)].astype(F32)
        a = jnp.where(core_at == 0, own, other)
        b = jnp.where(core_at == 0, other, own)
        first, second = mix(a, b)
        right_ref[:, block(2 * m)] = first.astype(BF16)
        right_ref[:, block(2 * m + 1)] = second.astype(BF16)
    for m in range(LINES // 2):
        tri = dot(right_ref[...], left_ref[:, block(m)], 0, 0)
        tri = tri.reshape(32, HALF, LANES)
        a = tri[:, 0:LOW, :].reshape(256, LANES)
        b = tri[:, LOW:HALF, :].reshape(256, LANES)
        first, second = mix(a, b)
        out_ref[pl.ds(2 * m * 256, 256), :] = first.astype(BF16)
        out_ref[pl.ds((2 * m + 1) * 256, 256), :] = second.astype(BF16)


def middle_kernel(
    tri_ref, grad_ref, x_ref, w_gate_ref, w_out_ref, gain_ref, bias_ref, out_ref, gate_grad_ref, tile, hats, turned
):
    slab_at = lax.axis_index("slab")
    load_half(grad_ref, slab_at, tile)
    parts = tri_ref[...].astype(F32).reshape(OWN, 2 * LOW, LANES)
    tri = jnp.concatenate([parts[:, 0:LOW, :], parts[:, LOW : 2 * LOW, :]], axis=0)
    average = jnp.mean(tri, axis=0, keepdims=True)
    centred = tri - average
    inv = lax.rsqrt(jnp.mean(centred * centred, axis=0, keepdims=True) + 1e-05)
    hats[...] = (centred * inv).reshape(CHANNELS * LOW, LANES)
    gain = jnp.broadcast_to(gain_ref[...], (CHANNELS, LANES)).T
    bias = jnp.broadcast_to(bias_ref[...], (CHANNELS, LANES)).T
    for low in range(LOW):
        here = pl.ds(low * LANES, LANES)
        hat = hats[pl.ds(low, CHANNELS, stride=LOW), :]
        mid_out = (hat * gain + bias).astype(BF16)
        proj_out = dot(mid_out, w_out_ref[...], 0, 0)
        gate = jax.nn.sigmoid(dot(x_ref[here, :], w_gate_ref[...], 1, 0))
        grad_in = jnp.concatenate([column(tile, low), column(tile, low + LOW)], axis=0)
        gate_grad_ref[here, :] = (grad_in * proj_out * gate * (1.0 - gate)).astype(BF16)
        mid_in_grad = (grad_in * gate).astype(BF16)
        grad_hat = dot(w_out_ref[...], mid_in_grad, 1, 1) * gain
        first = jnp.mean(grad_hat, axis=0, keepdims=True)
        second = jnp.mean(grad_hat * hat, axis=0, keepdims=True)
        tri_grad = (grad_hat - first - hat * second) * inv[0, low : low + 1, :]
        turned[pl.ds(low, CHANNELS, stride=LOW), :] = tri_grad
    done = turned[...].reshape(CHANNELS, LOW, LANES)
    both = jnp.concatenate([done[0:OWN], done[OWN:CHANNELS]], axis=1)
    out_ref[...] = both.astype(BF16).reshape(CHANNELS * LOW, LANES)


def grads_kernel(tri_grad_ref, left_ref, right_ref, left_grad_ref, own_ref, other_ref, grid_t):
    core_at = lax.axis_index("core")
    for m in range(LINES // 2):
        a = tri_grad_ref[pl.ds(2 * m * 256, 256), :].astype(F32)
        b = tri_grad_ref[pl.ds((2 * m + 1) * 256, 256), :].astype(F32)
        first, second = mix(a, b)
        both = jnp.concatenate(
            [first.reshape(32, LOW, LANES), second.reshape(32, LOW, LANES)], axis=1
        )
        grid_t[:, block(m)] = both.reshape(32 * HALF, LANES).astype(BF16)
    for m in range(LINES // 2):
        a = dot(left_ref[...], grid_t[pl.ds(2 * m * LANES, LANES), :], 1, 1)
        b = dot(left_ref[...], grid_t[pl.ds((2 * m + 1) * LANES, LANES), :], 1, 1)
        first, second = mix(a, b)
        own_ref[:, block(m)] = jnp.where(core_at == 0, first, second)
        other_ref[:, block(m)] = jnp.where(core_at == 0, second, first).astype(BF16)
    for m in range(LINES // 2):
        left_grad_ref[:, block(m)] = dot(right_ref[...], grid_t[:, block(m)], 1, 0)


def join_kernel(left_grad_ref, own_ref, other_ref, out_ref):
    for m in range(LINES // 2):
        right_grad = own_ref[:, block(m)] + other_ref[:, block(m)].astype(F32)
        first, second = mix(left_grad_ref[:, block(m)], right_grad)
        out_ref[pl.ds(2 * m * 512, 512), :] = first.astype(BF16)
        out_ref[pl.ds((2 * m + 1) * 512, 512), :] = second.astype(BF16)


def final_kernel(
    grads_ref, act_ref, x_ref, keep_ref, gate_grad_ref, w_proj_ref, w_gate_ref, gain_ref, out_ref,
    tile, grads, projected, proj_grad, x_grad, result,
):
    slab_at = lax.axis_index("slab")
    load_half(act_ref, slab_at, tile)
    grads[...] = grads_ref[...].astype(F32)
    projected[...] = dot(x_ref[...], w_proj_ref[...], 1, 0)
    for k in range(HALF):
        here = pl.ds(place(k), ROWS)
        both = jnp.concatenate(
            [grads[pl.ds(k + at, OWN, stride=2 * HALF), :] for at in (0, HALF)], axis=0
        )
        both = (both * keep_ref[k : k + 1, :]).T
        for side in range(2):
            grad = both[side * ROWS : (side + 1) * ROWS, :]
            at = side * 256
            sig = jax.nn.sigmoid(projected[here, at : at + 128])
            value = projected[here, at + 128 : at + 256]
            proj_grad[here, at : at + 128] = (grad * value * sig * (1.0 - sig)).astype(BF16)
            proj_grad[here, at + 128 : at + 256] = (grad * sig).astype(BF16)
    x_grad[...] = dot(proj_grad[...], w_proj_ref[...], 1, 1) + dot(gate_grad_ref[...], w_gate_ref[...], 1, 1)
    for k in range(HALF):
        normed, inv_std = normalize(column(tile, k))
        in_hat = x_grad[pl.ds(place(k), ROWS), :] * gain_ref[...]
        first = jnp.mean(in_hat, axis=-1, keepdims=True)
        second = jnp.mean(in_hat * normed, axis=-1, keepdims=True)
        result[pl.ds(k, ROWS, stride=HALF), :] = (in_hat - first - normed * second) * inv_std
    out_ref[...] = result[...].reshape(ROWS, HALF, LANES).astype(BF16)


SMEM = pl.BlockSpec(memory_space=pltpu.SMEM)
VMEM = pl.BlockSpec(memory_space=pltpu.VMEM)


def call(kernel, outs, scratch, args, name, smem=0):
    single = not isinstance(outs, list)
    return pl.pallas_call(
        kernel,
        out_shape=outs,
        in_specs=[SMEM] * smem + [VMEM] * (len(args) - smem),
        out_specs=VMEM if single else [VMEM] * len(outs),
        scratch_shapes=scratch,
        compiler_params=pltpu.CompilerParams(vmem_limit_bytes=24 * 1024 * 1024),
        name=name,
    )(*args)


def shape(dims, kind):
    return jax.ShapeDtypeStruct(dims, kind)


def exchange(flat, axes):
    pieces = lax.axis_size(axes)
    cut = flat.reshape(pieces, flat.shape[0] // pieces, LANES)
    return lax.all_to_all(cut, axes, 0, 0, tiled=True).reshape(flat.shape)


def swap(x):
    return lax.ppermute(x, "core", [(0, 1), (1, 0)])


def on_device(
    pair_act, out_grad, pair_mask, chain_starts, in_gain, in_bias, w_proj, w_gate, w_out, mid_gain, mid_bias
):
    in_gain, in_bias, mid_gain, mid_bias = (
        v.reshape(1, LANES) for v in (in_gain, in_bias, mid_gain, mid_bias)
    )
    edge_rows = OWN * COLS
    tri_rows = CHANNELS * LOW
    edges, x_in, keep = call(
        edges_kernel,
        [shape((edge_rows, LANES), BF16), shape((POINTS, LANES), BF16), shape((HALF, LANES), F32)],
        [
            pltpu.VMEM((2 * POINTS, LANES), F32),
            pltpu.VMEM((COLS, LANES), F32),
            pltpu.VMEM((2 * POINTS, LANES), BF16),
            pltpu.VMEM((2 * POINTS, 256), F32),
            pltpu.VMEM((edge_rows, LANES), F32),
        ],
        (chain_starts, pair_act, pair_mask, in_gain, in_bias, w_proj),
        "edges",
        smem=1,
    )
    edges = exchange(edges, NEAR)
    left, own = call(
        sort_kernel, [shape((512, 256), BF16), shape((512, 256), BF16)], [], (edges,), "sort"
    )
    tri, right = call(
        triangle_kernel,
        [shape((tri_rows, LANES), BF16), shape((512, 512), BF16)],
        [],
        (left, own, swap(own)),
        "triangle",
    )
    tri = exchange(tri, FAR)
    tri_grad, gate_grad = call(
        middle_kernel,
        [shape((tri_rows, LANES), BF16), shape((POINTS, LANES), BF16)],
        [
            pltpu.VMEM((POINTS, LANES), F32),
            pltpu.VMEM((tri_rows, LANES), F32),
            pltpu.VMEM((tri_rows, LANES), F32),
        ],
        (tri, out_grad, x_in, w_gate, w_out, mid_gain, mid_bias),
        "middle",
    )
    tri_grad = exchange(tri_grad, FAR)
    left_grad, own, other = call(
        grads_kernel,
        [shape((512, 256), F32), shape((512, 256), F32), shape((512, 256), BF16)],
        [pltpu.VMEM((512, 256), BF16)],
        (tri_grad, left, right),
        "grads",
    )
    grads = call(
        join_kernel, shape((CHANNELS * HALF, LANES), BF16), [], (left_grad, own, swap(other)), "join"
    )
    grads = exchange(grads, FAR)
    result = call(
        final_kernel,
        shape((ROWS, HALF, LANES), BF16),
        [
            pltpu.VMEM((POINTS, LANES), F32),
            pltpu.VMEM((CHANNELS * HALF, LANES), F32),
            pltpu.VMEM((POINTS, 512), F32),
            pltpu.VMEM((POINTS, 512), BF16),
            pltpu.VMEM((POINTS, LANES), F32),
            pltpu.VMEM((POINTS, LANES), F32),
        ],
        (grads, pair_act, x_in, keep, gate_grad, w_proj, w_gate, in_gain),
        "final",
    )
    return result.reshape(ROWS, 1, 1, HALF, LANES)


def solution(mesh):
    fine = Mesh(mesh.devices.reshape(2, LINES, 2, 4, 4), ("slab", "x", "core", "y", "z"))
    row, col = ("x", "core"), ("y", "z")
    in_specs = (P(row, col, None), P(row, col, None), P(row, col)) + (P(),) * 8
    out_specs = P(row, col, "slab", None, None)
    return jax.shard_map(
        on_device, mesh=fine, in_specs=in_specs, out_specs=out_specs, check_vma=False
    )
```

```python
import jax
import jax.numpy as jnp
from jax import lax
from jax.experimental import pallas as pl
from jax.experimental.pallas import tpu as pltpu
from jax.sharding import Mesh
from jax.sharding import PartitionSpec as P

BF16 = jnp.bfloat16
F32 = jnp.float32
LANES = 128
ROWS = 64
HALF = 16
COLS = 2 * HALF
LOW = 8
CHANNELS = 128
OWN = CHANNELS // 2
POINTS = ROWS * HALF
LINES = 4
NEAR = ("z", "x", "y")
FAR = ("z", "x", "y", "slab")


def dot(a, b, ca, cb):
    return lax.dot_general(a, b, (((ca,), (cb,)), ((), ())), preferred_element_type=F32)


def place(k):
    return ((k % LOW) * (HALF // LOW) + k // LOW) * ROWS


def normalize(values):
    average = jnp.mean(values, axis=-1, keepdims=True)
    centred = values - average
    inv_std = lax.rsqrt(jnp.mean(centred * centred, axis=-1, keepdims=True) + 1e-05)
    return centred * inv_std, inv_std


def mix(a, b):
    low = lax.broadcasted_iota(jnp.int32, a.shape, 1) < ROWS
    first = jnp.where(low, a, pltpu.roll(b, ROWS, 1))
    second = jnp.where(low, pltpu.roll(a, ROWS, 1), b)
    return first, second


def block(m):
    return slice(m * LANES, (m + 1) * LANES)


def load_half(ref, slab_at, scratch):
    start = pl.multiple_of(slab_at * HALF, HALF)
    scratch[...] = ref[:, pl.ds(start, HALF), :].astype(F32).reshape(POINTS, LANES)


def column(scratch, k, width=HALF):
    return scratch[pl.ds(k, ROWS, stride=width), :]


def two_columns(scratch, low):
    return jnp.concatenate([column(scratch, low), column(scratch, low + LOW)], axis=0)


def keep_rows(mask, starts_ref, row_at, col_at):
    wide = jnp.concatenate([mask, mask], axis=1)
    shape = (COLS, LANES)
    lane = lax.broadcasted_iota(jnp.int32, shape, 1)
    row_ids = row_at * ROWS + jnp.where(lane < ROWS, lane, lane - ROWS)
    col_ids = col_at * COLS + lax.broadcasted_iota(jnp.int32, shape, 0)
    row_chain = jnp.zeros(shape, jnp.int32)
    col_chain = jnp.zeros(shape, jnp.int32)
    for at in range(starts_ref.shape[0]):
        start_at = starts_ref[at]
        row_chain = row_chain + (row_ids >= start_at).astype(jnp.int32)
        col_chain = col_chain + (col_ids >= start_at).astype(jnp.int32)
    return jnp.where((row_chain == col_chain) | (wide > 0), 1.0, 0.0)


def halves(a, b):
    return jnp.where(lax.broadcasted_iota(jnp.int32, a.shape, 1) < ROWS, a, b)


def edges_kernel(
    starts_ref, act_ref, mask_ref, gain_ref, bias_ref, w_ref, edges_ref, x_ref, keep_ref,
    tile, kept, x_all, projected, turned,
):
    slab_at = lax.axis_index("slab")
    row_at = lax.axis_index("x") * 2 + lax.axis_index("core")
    col_at = lax.axis_index("y") * 4 + lax.axis_index("z")
    kept[...] = keep_rows(mask_ref[...], starts_ref, row_at, col_at)
    start = pl.multiple_of(slab_at * HALF, HALF)
    keep_ref[...] = halves(kept[pl.ds(start, LOW), :], kept[pl.ds(start + LOW, LOW), :])
    own = []
    for at in range(2):
        first, second = mix(w_ref[:, block(at)].astype(F32), w_ref[:, block(at + 2)].astype(F32))
        own.append(jnp.where(slab_at == 0, first, second).astype(BF16))
    w_own = jnp.concatenate(own, axis=1)
    tile[...] = act_ref[...].astype(F32).reshape(ROWS * COLS, LANES)
    for k in range(COLS):
        normed, _ = normalize(column(tile, k, COLS))
        at = (k % HALF * 2 + k // HALF) * ROWS
        x_all[pl.ds(at, ROWS), :] = (normed * gain_ref[...] + bias_ref[...]).astype(BF16)
    projected[...] = dot(w_own, x_all[...], 0, 1)
    for k in range(HALF):
        both = jax.nn.sigmoid(projected[0:128, block(k)]) * projected[128:256, block(k)]
        both = both * halves(kept[k : k + 1, :], kept[k + HALF : k + HALF + 1, :])
        turned[pl.ds(k, OWN, stride=COLS), :] = both[0:OWN, :]
        turned[pl.ds(k + HALF, OWN, stride=COLS), :] = both[OWN:CHANNELS, :]
    edges_ref[...] = turned[...].astype(BF16)
    for k in range(HALF):
        mine = pl.multiple_of(2 * k * ROWS + slab_at * ROWS, ROWS)
        x_ref[pl.ds(place(k), ROWS), :] = x_all[pl.ds(mine, ROWS), :]


def ahead_kernel(
    act_ref, grad_ref, x_ref, keep_ref, w_proj_ref, w_gate_ref, w_out_ref, gain_ref, in_gain_ref,
    slope_ref, grad_hat_ref, factor_ref, normed_ref, inv_ref, tall_gain_ref, tile, projected,
):
    tall_gain_ref[...] = jnp.broadcast_to(in_gain_ref[...], (LANES, LANES)).T
    slab_at = lax.axis_index("slab")
    load_half(grad_ref, slab_at, tile)
    gain = jnp.broadcast_to(gain_ref[...], (CHANNELS, LANES)).T
    for low in range(LOW):
        here = pl.ds(low * LANES, LANES)
        gate = jax.nn.sigmoid(dot(x_ref[here, :], w_gate_ref[...], 1, 0))
        grad_in = two_columns(tile, low)
        slope_ref[here, :] = grad_in * gate * (1.0 - gate)
        mid_in_grad = (grad_in * gate).astype(BF16)
        grad_hat = dot(w_out_ref[...], mid_in_grad, 1, 1) * gain
        grad_hat_ref[pl.ds(low, CHANNELS, stride=LOW), :] = grad_hat - jnp.mean(grad_hat, axis=0, keepdims=True)
    load_half(act_ref, slab_at, tile)
    for low in range(LOW):
        values = two_columns(tile, low).T
        centred = values - jnp.mean(values, axis=0, keepdims=True)
        inv = lax.rsqrt(jnp.mean(centred * centred, axis=0, keepdims=True) + 1e-05)
        normed_ref[:, block(low)] = centred * inv
        inv_ref[:, block(low)] = inv
    projected[...] = dot(w_proj_ref[...], x_ref[...], 0, 1)
    for low in range(LOW):
        keep = keep_ref[low : low + 1, :]
        for side in range(2):
            at = side * 256
            sig = jax.nn.sigmoid(projected[at : at + 128, block(low)])
            value = projected[at + 128 : at + 256, block(low)]
            factor_ref[at : at + 128, block(low)] = (keep * value * sig * (1.0 - sig)).astype(BF16)
            factor_ref[at + 128 : at + 256, block(low)] = (keep * sig).astype(BF16)


def sort_kernel(edges_ref, left_ref, right_ref):
    for m in range(LINES // 2):
        for side, ref in enumerate((left_ref, right_ref)):
            a, b = (
                jnp.concatenate(
                    [
                        edges_ref[pl.ds((z * 16 + x * 4 + y) * COLS + side * HALF, HALF), :].astype(F32)
                        for z in range(LINES)
                        for y in range(LINES)
                    ],
                    axis=0,
                )
                for x in (2 * m, 2 * m + 1)
            )
            first, second = mix(a, b)
            both = jnp.concatenate(
                [first.reshape(16, HALF, LANES), second.reshape(16, HALF, LANES)], axis=1
            )
            ref[:, block(m)] = both.reshape(512, LANES).astype(BF16)


def triangle_kernel(left_ref, own_ref, other_ref, out_ref, right_ref):
    core_at = lax.axis_index("core")
    for m in range(LINES // 2):
        own, other = own_ref[:, block(m)].astype(F32), other_ref[:, block(m)].astype(F32)
        a = jnp.where(core_at == 0, own, other)
        b = jnp.where(core_at == 0, other, own)
        first, second = mix(a, b)
        right_ref[:, block(2 * m)] = first.astype(BF16)
        right_ref[:, block(2 * m + 1)] = second.astype(BF16)
    for m in range(LINES // 2):
        tri = dot(right_ref[...], left_ref[:, block(m)], 0, 0)
        tri = tri.reshape(32, HALF, LANES)
        a = tri[:, 0:LOW, :].reshape(256, LANES)
        b = tri[:, LOW:HALF, :].reshape(256, LANES)
        for x, part in zip((2 * m, 2 * m + 1), mix(a, b)):
            part = part.reshape(LINES, LINES, HALF, LANES)
            for z in range(LINES):
                out_ref[pl.ds((z * 4 + x) * 64, 64), :] = part[:, z].reshape(64, LANES).astype(BF16)


def middle_kernel(tri_ref, grad_hat_ref, out_ref, hats_ref):
    parts = tri_ref[...].astype(F32).reshape(OWN, 2 * LOW, LANES)
    tri = jnp.concatenate([parts[:, 0:LOW, :], parts[:, LOW : 2 * LOW, :]], axis=0)
    average = jnp.mean(tri, axis=0, keepdims=True)
    centred = tri - average
    inv = lax.rsqrt(jnp.mean(centred * centred, axis=0, keepdims=True) + 1e-05)
    hat = centred * inv
    hats_ref[...] = hat.reshape(CHANNELS * LOW, LANES)
    grad_hat = grad_hat_ref[...].reshape(CHANNELS, LOW, LANES)
    second = jnp.mean(grad_hat * hat, axis=0, keepdims=True)
    done = (grad_hat - hat * second) * inv
    both = jnp.concatenate([done[0:OWN], done[OWN:CHANNELS]], axis=1)
    out_ref[...] = both.astype(BF16).reshape(CHANNELS * LOW, LANES)


def late_kernel(hats_ref, slope_ref, w_gate_ref, w_out_ref, gain_ref, bias_ref, out_ref):
    gain = jnp.broadcast_to(gain_ref[...], (CHANNELS, LANES)).T
    bias = jnp.broadcast_to(bias_ref[...], (CHANNELS, LANES)).T
    for low in range(LOW):
        hat = hats_ref[pl.ds(low, CHANNELS, stride=LOW), :]
        mid_out = (hat * gain + bias).astype(BF16)
        proj_out = dot(mid_out, w_out_ref[...], 0, 0)
        gate_grad = (slope_ref[pl.ds(low * LANES, LANES), :] * proj_out).astype(BF16)
        out_ref[:, block(low)] = dot(w_gate_ref[...], gate_grad, 1, 1)


def grads_kernel(tri_grad_ref, left_ref, right_ref, left_grad_ref, own_ref, other_ref, grid_t):
    core_at = lax.axis_index("core")
    for m in range(LINES // 2):
        a, b = (
            jnp.concatenate(
                [
                    tri_grad_ref[pl.ds((z * 16 + x * 4 + y) * HALF, HALF), :].astype(F32)
                    for y in range(LINES)
                    for z in range(LINES)
                ],
                axis=0,
            )
            for x in (2 * m, 2 * m + 1)
        )
        first, second = mix(a, b)
        both = jnp.concatenate(
            [first.reshape(32, LOW, LANES), second.reshape(32, LOW, LANES)], axis=1
        )
        grid_t[:, block(m)] = both.reshape(32 * HALF, LANES).astype(BF16)
    for m in range(LINES // 2):
        a = dot(left_ref[...], grid_t[pl.ds(2 * m * LANES, LANES), :], 1, 1)
        b = dot(left_ref[...], grid_t[pl.ds((2 * m + 1) * LANES, LANES), :], 1, 1)
        first, second = mix(a, b)
        own_ref[:, block(m)] = jnp.where(core_at == 0, first, second)
        other_ref[:, block(m)] = jnp.where(core_at == 0, second, first).astype(BF16)
    for m in range(LINES // 2):
        left_grad_ref[:, block(m)] = dot(right_ref[...], grid_t[:, block(m)], 1, 0)


def join_kernel(left_grad_ref, own_ref, other_ref, out_ref):
    for m in range(LINES // 2):
        left_grad = left_grad_ref[:, block(m)]
        right_grad = own_ref[:, block(m)] + other_ref[:, block(m)].astype(F32)
        sides = []
        for grad in (left_grad, right_grad):
            grad = grad.reshape(32, HALF, LANES)
            a = grad[:, 0:LOW, :].reshape(256, LANES)
            b = grad[:, LOW:HALF, :].reshape(256, LANES)
            sides.append([part.reshape(32, LOW, LANES) for part in mix(a, b)])
        for at, x in enumerate((2 * m, 2 * m + 1)):
            both = jnp.concatenate([sides[0][at], sides[1][at]], axis=1)
            both = both.astype(BF16).reshape(512, LANES)
            for z in range(LINES):
                out_ref[pl.ds((z * 4 + x) * LANES, LANES), :] = both[z * LANES : (z + 1) * LANES]


def final_kernel(
    grads_ref, factor_ref, part_ref, normed_ref, inv_ref, w_proj_ref, tall_gain_ref, out_ref,
    grads, proj_grad, result,
):
    grads[...] = grads_ref[...].astype(F32)
    for low in range(LOW):
        for side in range(2):
            grad = jnp.concatenate(
                [
                    grads[pl.ds(slab * HALF + side * LOW + low, OWN, stride=2 * HALF), :]
                    for slab in range(2)
                ],
                axis=0,
            )
            for at in (side * 256, side * 256 + 128):
                factor = factor_ref[at : at + 128, block(low)].astype(F32)
                proj_grad[at : at + 128, block(low)] = (grad * factor).astype(BF16)
    gain = tall_gain_ref[...]
    for low in range(LOW):
        x_grad = dot(w_proj_ref[...], proj_grad[:, block(low)], 1, 0) + part_ref[:, block(low)]
        normed = normed_ref[:, block(low)]
        in_hat = x_grad * gain
        first = jnp.mean(in_hat, axis=0, keepdims=True)
        second = jnp.mean(in_hat * normed, axis=0, keepdims=True)
        done = ((in_hat - first - normed * second) * inv_ref[:, block(low)]).T
        result[pl.ds(low, ROWS, stride=HALF), :] = done[0:ROWS, :]
        result[pl.ds(low + LOW, ROWS, stride=HALF), :] = done[ROWS:LANES, :]
    out_ref[...] = result[...].reshape(ROWS, HALF, LANES).astype(BF16)


SMEM = pl.BlockSpec(memory_space=pltpu.SMEM)
VMEM = pl.BlockSpec(memory_space=pltpu.VMEM)


def call(kernel, outs, scratch, args, name, smem=0, cost=None, room=24):
    single = not isinstance(outs, list)
    return pl.pallas_call(
        kernel,
        out_shape=outs,
        in_specs=[SMEM] * smem + [VMEM] * (len(args) - smem),
        out_specs=VMEM if single else [VMEM] * len(outs),
        scratch_shapes=scratch,
        compiler_params=pltpu.CompilerParams(vmem_limit_bytes=room * 1024 * 1024),
        cost_estimate=cost,
        name=name,
    )(*args)


def shape(dims, kind):
    return jax.ShapeDtypeStruct(dims, kind)


def exchange(flat, axes):
    pieces = lax.axis_size(axes)
    cut = flat.reshape(pieces, flat.shape[0] // pieces, LANES)
    return lax.all_to_all(cut, axes, 0, 0, tiled=True).reshape(flat.shape)


def swap(x):
    return lax.ppermute(x, "core", [(0, 1), (1, 0)])


def on_device(
    pair_act, out_grad, pair_mask, chain_starts, in_gain, in_bias, w_proj, w_gate, w_out, mid_gain, mid_bias
):
    in_gain, in_bias, mid_gain, mid_bias = (
        v.reshape(1, LANES) for v in (in_gain, in_bias, mid_gain, mid_bias)
    )
    edge_rows = OWN * COLS
    tri_rows = CHANNELS * LOW
    edges, x_in, keep = call(
        edges_kernel,
        [shape((edge_rows, LANES), BF16), shape((POINTS, LANES), BF16), shape((LOW, LANES), F32)],
        [
            pltpu.VMEM((2 * POINTS, LANES), F32),
            pltpu.VMEM((COLS, LANES), F32),
            pltpu.VMEM((2 * POINTS, LANES), BF16),
            pltpu.VMEM((256, 2 * POINTS), F32),
            pltpu.VMEM((edge_rows, LANES), F32),
        ],
        (chain_starts, pair_act, pair_mask.T, in_gain, in_bias, w_proj),
        "edges",
        smem=1,
        room=63,
    )
    edges = exchange(edges, NEAR)
    slope, grad_hat, factor, normed, inv, tall_gain = call(
        ahead_kernel,
        [
            shape((POINTS, LANES), F32),
            shape((tri_rows, LANES), F32),
            shape((512, POINTS), BF16),
            shape((LANES, POINTS), F32),
            shape((1, POINTS), F32),
            shape((LANES, LANES), F32),
        ],
        [pltpu.VMEM((POINTS, LANES), F32), pltpu.VMEM((512, POINTS), F32)],
        (pair_act, out_grad, x_in, keep, w_proj, w_gate, w_out, mid_gain, in_gain),
        "ahead",
        cost=pl.CostEstimate(flops=300_000_000, bytes_accessed=6_000_000, transcendentals=700_000),
    )
    edges, slope, grad_hat, factor, normed, inv, tall_gain = lax.optimization_barrier(
        (edges, slope, grad_hat, factor, normed, inv, tall_gain)
    )
    left, own = call(
        sort_kernel, [shape((512, 256), BF16), shape((512, 256), BF16)], [], (edges,), "sort"
    )
    tri, right = call(
        triangle_kernel,
        [shape((tri_rows, LANES), BF16), shape((512, 512), BF16)],
        [],
        (left, own, swap(own)),
        "triangle",
    )
    tri = exchange(tri, FAR)
    tri_grad, hats = call(
        middle_kernel,
        [shape((tri_rows, LANES), BF16), shape((tri_rows, LANES), F32)],
        [],
        (tri, grad_hat),
        "middle",
    )
    tri_grad = exchange(tri_grad, FAR)
    left_grad, own, other = call(
        grads_kernel,
        [shape((512, 256), F32), shape((512, 256), F32), shape((512, 256), BF16)],
        [pltpu.VMEM((512, 256), BF16)],
        (tri_grad, left, right),
        "grads",
    )
    other, hats = lax.optimization_barrier((other, hats))
    swapped = swap(other)
    part = call(
        late_kernel,
        shape((LANES, POINTS), F32),
        [],
        (hats, slope, w_gate, w_out, mid_gain, mid_bias),
        "late",
        cost=pl.CostEstimate(flops=70_000_000, bytes_accessed=2_000_000, transcendentals=0),
    )
    swapped, part = lax.optimization_barrier((swapped, part))
    grads = call(
        join_kernel, shape((CHANNELS * HALF, LANES), BF16), [], (left_grad, own, swapped), "join"
    )
    grads = exchange(grads, FAR)
    result = call(
        final_kernel,
        shape((ROWS, HALF, LANES), BF16),
        [
            pltpu.VMEM((CHANNELS * HALF, LANES), F32),
            pltpu.VMEM((512, POINTS), BF16),
            pltpu.VMEM((POINTS, LANES), F32),
        ],
        (grads, factor, part, normed, inv, w_proj, tall_gain),
        "final",
    )
    return result.reshape(ROWS, 1, 1, HALF, LANES)


def solution(mesh):
    fine = Mesh(mesh.devices.reshape(2, LINES, 2, 4, 4), ("slab", "x", "core", "y", "z"))
    row, col = ("x", "core"), ("y", "z")
    in_specs = (P(row, col, None), P(row, col, None), P(row, col)) + (P(),) * 8
    out_specs = P(row, col, "slab", None, None)
    return jax.shard_map(
        on_device, mesh=fine, in_specs=in_specs, out_specs=out_specs, check_vma=False
    )
```

```python
import jax
import jax.numpy as jnp
from jax import lax
from jax.experimental import pallas as pl
from jax.experimental.pallas import tpu as pltpu
from jax.sharding import Mesh
from jax.sharding import PartitionSpec as P

BF16 = jnp.bfloat16
F32 = jnp.float32
LANES = 128
ROWS = 64
HALF = 16
COLS = 2 * HALF
LOW = 8
CHANNELS = 128
OWN = CHANNELS // 2
POINTS = ROWS * HALF
PITCH = COLS + 8
STEP = HALF + 8
LINES = 4
NEAR = ("z", "x", "y")
FAR = ("z", "x", "y", "slab")


def dot(a, b, ca, cb):
    return lax.dot_general(a, b, (((ca,), (cb,)), ((), ())), preferred_element_type=F32)


def place(k):
    return ((k % LOW) * (HALF // LOW) + k // LOW) * ROWS


def normalize(values):
    average = jnp.mean(values, axis=-1, keepdims=True)
    centred = values - average
    inv_std = lax.rsqrt(jnp.mean(centred * centred, axis=-1, keepdims=True) + 1e-05)
    return centred * inv_std, inv_std


def mix(a, b):
    low = lax.broadcasted_iota(jnp.int32, a.shape, 1) < ROWS
    first = jnp.where(low, a, pltpu.roll(b, ROWS, 1))
    second = jnp.where(low, pltpu.roll(a, ROWS, 1), b)
    return first, second


def block(m):
    return slice(m * LANES, (m + 1) * LANES)


def load_half(ref, slab_at, scratch):
    start = pl.multiple_of(slab_at * HALF, HALF)
    scratch[...] = ref[:, pl.ds(start, HALF), :].astype(F32).reshape(POINTS, LANES)


def column(scratch, k, width=HALF):
    return scratch[pl.ds(k, ROWS, stride=width), :]


def two_columns(scratch, low):
    return jnp.concatenate([column(scratch, low), column(scratch, low + LOW)], axis=0)


def keep_rows(mask, starts_ref, row_at, col_at):
    wide = jnp.concatenate([mask, mask], axis=1)
    shape = (COLS, LANES)
    lane = lax.broadcasted_iota(jnp.int32, shape, 1)
    row_ids = row_at * ROWS + jnp.where(lane < ROWS, lane, lane - ROWS)
    col_ids = col_at * COLS + lax.broadcasted_iota(jnp.int32, shape, 0)
    row_chain = jnp.zeros(shape, jnp.int32)
    col_chain = jnp.zeros(shape, jnp.int32)
    for at in range(starts_ref.shape[0]):
        start_at = starts_ref[at]
        row_chain = row_chain + (row_ids >= start_at).astype(jnp.int32)
        col_chain = col_chain + (col_ids >= start_at).astype(jnp.int32)
    return jnp.where((row_chain == col_chain) | (wide > 0), 1.0, 0.0)


def halves(a, b):
    return jnp.where(lax.broadcasted_iota(jnp.int32, a.shape, 1) < ROWS, a, b)


def edges_kernel(
    starts_ref, act_ref, mask_ref, gain_ref, bias_ref, w_ref, edges_ref, x_ref, keep_ref,
    tile, kept, x_all, projected, turned,
):
    slab_at = lax.axis_index("slab")
    row_at = lax.axis_index("x") * 2 + lax.axis_index("core")
    col_at = lax.axis_index("y") * 4 + lax.axis_index("z")
    kept[...] = keep_rows(mask_ref[...], starts_ref, row_at, col_at)
    start = pl.multiple_of(slab_at * HALF, HALF)
    keep_ref[...] = halves(kept[pl.ds(start, LOW), :], kept[pl.ds(start + LOW, LOW), :])
    own = []
    for at in range(2):
        first, second = mix(w_ref[:, block(at)].astype(F32), w_ref[:, block(at + 2)].astype(F32))
        own.append(jnp.where(slab_at == 0, first, second).astype(BF16))
    w_own = jnp.concatenate(own, axis=1)
    values = act_ref[...].astype(F32)
    spare = jnp.zeros((ROWS, PITCH - COLS, LANES), F32)
    tile[...] = jnp.concatenate([values, spare], axis=1).reshape(ROWS * PITCH, LANES)
    for k in range(COLS):
        normed, _ = normalize(column(tile, k, PITCH))
        at = (k % HALF * 2 + k // HALF) * ROWS
        x_all[pl.ds(at, ROWS), :] = (normed * gain_ref[...] + bias_ref[...]).astype(BF16)
    projected[...] = dot(w_own, x_all[...], 0, 1)
    for k in range(HALF):
        both = jax.nn.sigmoid(projected[0:128, block(k)]) * projected[128:256, block(k)]
        both = both * halves(kept[k : k + 1, :], kept[k + HALF : k + HALF + 1, :])
        turned[pl.ds(k, OWN, stride=PITCH), :] = both[0:OWN, :]
        turned[pl.ds(k + HALF, OWN, stride=PITCH), :] = both[OWN:CHANNELS, :]
    done = turned[...].reshape(OWN, PITCH, LANES)[:, 0:COLS, :]
    edges_ref[...] = done.reshape(OWN * COLS, LANES).astype(BF16)
    for k in range(HALF):
        mine = pl.multiple_of(2 * k * ROWS + slab_at * ROWS, ROWS)
        x_ref[pl.ds(place(k), ROWS), :] = x_all[pl.ds(mine, ROWS), :]


def ahead_kernel(
    act_ref, grad_ref, x_ref, keep_ref, w_proj_ref, w_gate_ref, w_out_ref, gain_ref, bias_ref, in_gain_ref,
    slope_ref, grad_hat_ref, factor_ref, normed_ref, inv_ref, tall_ref, tile, projected,
):
    for at, ref in enumerate((in_gain_ref, gain_ref, bias_ref)):
        tall_ref[at] = jnp.broadcast_to(ref[...], (LANES, LANES)).T
    slab_at = lax.axis_index("slab")
    load_half(grad_ref, slab_at, tile)
    gain = tall_ref[1]
    for low in range(LOW):
        here = pl.ds(low * LANES, LANES)
        gate = jax.nn.sigmoid(dot(x_ref[here, :], w_gate_ref[...], 1, 0))
        grad_in = two_columns(tile, low)
        slope_ref[here, :] = grad_in * gate * (1.0 - gate)
        mid_in_grad = (grad_in * gate).astype(BF16)
        grad_hat = dot(w_out_ref[...], mid_in_grad, 1, 1) * gain
        grad_hat_ref[pl.ds(low, CHANNELS, stride=LOW), :] = grad_hat - jnp.mean(grad_hat, axis=0, keepdims=True)
    load_half(act_ref, slab_at, tile)
    for low in range(LOW):
        values = two_columns(tile, low).T
        centred = values - jnp.mean(values, axis=0, keepdims=True)
        inv = lax.rsqrt(jnp.mean(centred * centred, axis=0, keepdims=True) + 1e-05)
        normed_ref[:, block(low)] = centred * inv
        inv_ref[:, block(low)] = inv
    projected[...] = dot(w_proj_ref[...], x_ref[...], 0, 1)
    for low in range(LOW):
        keep = keep_ref[low : low + 1, :]
        for side in range(2):
            at = side * 256
            sig = jax.nn.sigmoid(projected[at : at + 128, block(low)])
            value = projected[at + 128 : at + 256, block(low)]
            factor_ref[at : at + 128, block(low)] = (keep * value * sig * (1.0 - sig)).astype(BF16)
            factor_ref[at + 128 : at + 256, block(low)] = (keep * sig).astype(BF16)


def sort_kernel(edges_ref, left_ref, right_ref):
    for m in range(LINES // 2):
        for side, ref in enumerate((left_ref, right_ref)):
            a, b = (
                jnp.concatenate(
                    [
                        edges_ref[pl.ds((z * 16 + x * 4 + y) * COLS + side * HALF, HALF), :].astype(F32)
                        for z in range(LINES)
                        for y in range(LINES)
                    ],
                    axis=0,
                )
                for x in (2 * m, 2 * m + 1)
            )
            first, second = mix(a, b)
            both = jnp.concatenate(
                [first.reshape(16, HALF, LANES), second.reshape(16, HALF, LANES)], axis=1
            )
            ref[:, block(m)] = both.reshape(512, LANES).astype(BF16)


def triangle_kernel(left_ref, own_ref, other_ref, out_ref, right_ref):
    core_at = lax.axis_index("core")
    for m in range(LINES // 2):
        own, other = own_ref[:, block(m)].astype(F32), other_ref[:, block(m)].astype(F32)
        a = jnp.where(core_at == 0, own, other)
        b = jnp.where(core_at == 0, other, own)
        first, second = mix(a, b)
        right_ref[:, block(2 * m)] = first.astype(BF16)
        right_ref[:, block(2 * m + 1)] = second.astype(BF16)
    for m in range(LINES // 2):
        tri = dot(right_ref[...], left_ref[:, block(m)], 0, 0)
        tri = tri.reshape(32, HALF, LANES)
        a = tri[:, 0:LOW, :].reshape(256, LANES)
        b = tri[:, LOW:HALF, :].reshape(256, LANES)
        for x, part in zip((2 * m, 2 * m + 1), mix(a, b)):
            part = part.reshape(LINES, LINES, HALF, LANES)
            for z in range(LINES):
                out_ref[pl.ds((z * 4 + x) * 64, 64), :] = part[:, z].reshape(64, LANES).astype(BF16)


def middle_kernel(tri_ref, grad_hat_ref, out_ref, hats_ref):
    parts = tri_ref[...].astype(F32).reshape(OWN, 2 * LOW, LANES)
    tri = jnp.concatenate([parts[:, 0:LOW, :], parts[:, LOW : 2 * LOW, :]], axis=0)
    average = jnp.mean(tri, axis=0, keepdims=True)
    centred = tri - average
    inv = lax.rsqrt(jnp.mean(centred * centred, axis=0, keepdims=True) + 1e-05)
    hat = centred * inv
    hats_ref[...] = hat.reshape(CHANNELS * LOW, LANES)
    grad_hat = grad_hat_ref[...].reshape(CHANNELS, LOW, LANES)
    second = jnp.mean(grad_hat * hat, axis=0, keepdims=True)
    done = (grad_hat - hat * second) * inv
    both = jnp.concatenate([done[0:OWN], done[OWN:CHANNELS]], axis=1)
    out_ref[...] = both.astype(BF16).reshape(CHANNELS * LOW, LANES)


def late_kernel(
    hats_ref, slope_ref, w_gate_ref, w_out_ref, tall_ref, right_ref, grid_t_ref, out_ref, left_grad_ref
):
    left_grad_ref[...] = dot(right_ref[...], grid_t_ref[...], 1, 0)
    gain, bias = tall_ref[1], tall_ref[2]
    for low in range(LOW):
        hat = hats_ref[pl.ds(low, CHANNELS, stride=LOW), :]
        mid_out = (hat * gain + bias).astype(BF16)
        proj_out = dot(mid_out, w_out_ref[...], 0, 0)
        gate_grad = (slope_ref[pl.ds(low * LANES, LANES), :] * proj_out).astype(BF16)
        out_ref[:, block(low)] = dot(w_gate_ref[...], gate_grad, 1, 1)


def grads_kernel(tri_grad_ref, left_ref, own_ref, other_ref, grid_t):
    core_at = lax.axis_index("core")
    for m in range(LINES // 2):
        a, b = (
            jnp.concatenate(
                [
                    tri_grad_ref[pl.ds((z * 16 + x * 4 + y) * HALF, HALF), :].astype(F32)
                    for y in range(LINES)
                    for z in range(LINES)
                ],
                axis=0,
            )
            for x in (2 * m, 2 * m + 1)
        )
        first, second = mix(a, b)
        both = jnp.concatenate(
            [first.reshape(32, LOW, LANES), second.reshape(32, LOW, LANES)], axis=1
        )
        grid_t[:, block(m)] = both.reshape(32 * HALF, LANES).astype(BF16)
    for m in range(LINES // 2):
        a = dot(left_ref[...], grid_t[pl.ds(2 * m * LANES, LANES), :], 1, 1)
        b = dot(left_ref[...], grid_t[pl.ds((2 * m + 1) * LANES, LANES), :], 1, 1)
        first, second = mix(a, b)
        own_ref[:, block(m)] = jnp.where(core_at == 0, first, second)
        other_ref[:, block(m)] = jnp.where(core_at == 0, second, first).astype(BF16)


def join_kernel(left_grad_ref, own_ref, other_ref, out_ref):
    for m in range(LINES // 2):
        left_grad = left_grad_ref[:, block(m)]
        right_grad = own_ref[:, block(m)] + other_ref[:, block(m)].astype(F32)
        sides = []
        for grad in (left_grad, right_grad):
            grad = grad.reshape(32, HALF, LANES)
            a = grad[:, 0:LOW, :].reshape(256, LANES)
            b = grad[:, LOW:HALF, :].reshape(256, LANES)
            sides.append([part.reshape(32, LOW, LANES) for part in mix(a, b)])
        for at, x in enumerate((2 * m, 2 * m + 1)):
            both = jnp.concatenate([sides[0][at], sides[1][at]], axis=1)
            both = both.astype(BF16).reshape(512, LANES)
            for z in range(LINES):
                out_ref[pl.ds((z * 4 + x) * LANES, LANES), :] = both[z * LANES : (z + 1) * LANES]


def final_kernel(
    grads_ref, factor_ref, part_ref, normed_ref, inv_ref, w_proj_ref, tall_ref, out_ref,
    grads, proj_grad, result,
):
    got = grads_ref[...].astype(F32).reshape(OWN, 2, HALF, LANES)
    spare = jnp.zeros((OWN, STEP - HALF, LANES), F32)
    for slab in range(2):
        part = jnp.concatenate([got[:, slab], spare], axis=1)
        grads[pl.ds(slab * OWN * STEP, OWN * STEP), :] = part.reshape(OWN * STEP, LANES)
    for low in range(LOW):
        for side in range(2):
            grad = jnp.concatenate(
                [
                    grads[pl.ds(slab * OWN * STEP + side * LOW + low, OWN, stride=STEP), :]
                    for slab in range(2)
                ],
                axis=0,
            )
            for at in (side * 256, side * 256 + 128):
                factor = factor_ref[at : at + 128, block(low)].astype(F32)
                proj_grad[at : at + 128, block(low)] = (grad * factor).astype(BF16)
    gain = tall_ref[0]
    for low in range(LOW):
        x_grad = dot(w_proj_ref[...], proj_grad[:, block(low)], 1, 0) + part_ref[:, block(low)]
        normed = normed_ref[:, block(low)]
        in_hat = x_grad * gain
        first = jnp.mean(in_hat, axis=0, keepdims=True)
        second = jnp.mean(in_hat * normed, axis=0, keepdims=True)
        done = ((in_hat - first - normed * second) * inv_ref[:, block(low)]).T
        result[pl.ds(low, ROWS, stride=STEP), :] = done[0:ROWS, :]
        result[pl.ds(low + LOW, ROWS, stride=STEP), :] = done[ROWS:LANES, :]
    out_ref[...] = result[...].reshape(ROWS, STEP, LANES)[:, 0:HALF, :].astype(BF16)


SMEM = pl.BlockSpec(memory_space=pltpu.SMEM)
VMEM = pl.BlockSpec(memory_space=pltpu.VMEM)


def call(kernel, outs, scratch, args, name, smem=0, cost=None, room=24):
    single = not isinstance(outs, list)
    return pl.pallas_call(
        kernel,
        out_shape=outs,
        in_specs=[SMEM] * smem + [VMEM] * (len(args) - smem),
        out_specs=VMEM if single else [VMEM] * len(outs),
        scratch_shapes=scratch,
        compiler_params=pltpu.CompilerParams(vmem_limit_bytes=room * 1024 * 1024),
        cost_estimate=cost,
        name=name,
    )(*args)


def shape(dims, kind):
    return jax.ShapeDtypeStruct(dims, kind)


def exchange(flat, axes):
    pieces = lax.axis_size(axes)
    cut = flat.reshape(pieces, flat.shape[0] // pieces, LANES)
    return lax.all_to_all(cut, axes, 0, 0, tiled=True).reshape(flat.shape)


def swap(x):
    return lax.ppermute(x, "core", [(0, 1), (1, 0)])


def on_device(
    pair_act, out_grad, pair_mask, chain_starts, in_gain, in_bias, w_proj, w_gate, w_out, mid_gain, mid_bias
):
    in_gain, in_bias, mid_gain, mid_bias = (
        v.reshape(1, LANES) for v in (in_gain, in_bias, mid_gain, mid_bias)
    )
    edge_rows = OWN * COLS
    tri_rows = CHANNELS * LOW
    edges, x_in, keep = call(
        edges_kernel,
        [shape((edge_rows, LANES), BF16), shape((POINTS, LANES), BF16), shape((LOW, LANES), F32)],
        [
            pltpu.VMEM((ROWS * PITCH, LANES), F32),
            pltpu.VMEM((COLS, LANES), F32),
            pltpu.VMEM((2 * POINTS, LANES), BF16),
            pltpu.VMEM((256, 2 * POINTS), F32),
            pltpu.VMEM((OWN * PITCH, LANES), F32),
        ],
        (chain_starts, pair_act, pair_mask.T, in_gain, in_bias, w_proj),
        "edges",
        smem=1,
        room=63,
    )
    edges = exchange(edges, NEAR)
    slope, grad_hat, factor, normed, inv, tall = call(
        ahead_kernel,
        [
            shape((POINTS, LANES), F32),
            shape((tri_rows, LANES), F32),
            shape((512, POINTS), BF16),
            shape((LANES, POINTS), F32),
            shape((1, POINTS), F32),
            shape((3, LANES, LANES), F32),
        ],
        [pltpu.VMEM((POINTS, LANES), F32), pltpu.VMEM((512, POINTS), F32)],
        (pair_act, out_grad, x_in, keep, w_proj, w_gate, w_out, mid_gain, mid_bias, in_gain),
        "ahead",
        cost=pl.CostEstimate(flops=300_000_000, bytes_accessed=6_000_000, transcendentals=700_000),
    )
    edges, slope, grad_hat, factor, normed, inv, tall = lax.optimization_barrier(
        (edges, slope, grad_hat, factor, normed, inv, tall)
    )
    left, own = call(
        sort_kernel, [shape((512, 256), BF16), shape((512, 256), BF16)], [], (edges,), "sort"
    )
    tri, right = call(
        triangle_kernel,
        [shape((tri_rows, LANES), BF16), shape((512, 512), BF16)],
        [],
        (left, own, swap(own)),
        "triangle",
    )
    tri = exchange(tri, FAR)
    tri_grad, hats = call(
        middle_kernel,
        [shape((tri_rows, LANES), BF16), shape((tri_rows, LANES), F32)],
        [],
        (tri, grad_hat),
        "middle",
    )
    tri_grad = exchange(tri_grad, FAR)
    own, other, grid_t = call(
        grads_kernel,
        [shape((512, 256), F32), shape((512, 256), BF16), shape((512, 256), BF16)],
        [],
        (tri_grad, left),
        "grads",
    )
    other, hats, grid_t = lax.optimization_barrier((other, hats, grid_t))
    swapped = swap(other)
    part, left_grad = call(
        late_kernel,
        [shape((LANES, POINTS), F32), shape((512, 256), F32)],
        [],
        (hats, slope, w_gate, w_out, tall, right, grid_t),
        "late",
        cost=pl.CostEstimate(flops=210_000_000, bytes_accessed=3_000_000, transcendentals=0),
    )
    swapped, part, left_grad = lax.optimization_barrier((swapped, part, left_grad))
    grads = call(
        join_kernel, shape((CHANNELS * HALF, LANES), BF16), [], (left_grad, own, swapped), "join"
    )
    grads = exchange(grads, FAR)
    result = call(
        final_kernel,
        shape((ROWS, HALF, LANES), BF16),
        [
            pltpu.VMEM((CHANNELS * STEP, LANES), F32),
            pltpu.VMEM((512, POINTS), BF16),
            pltpu.VMEM((ROWS * STEP, LANES), F32),
        ],
        (grads, factor, part, normed, inv, w_proj, tall),
        "final",
    )
    return result.reshape(ROWS, 1, 1, HALF, LANES)


def solution(mesh):
    fine = Mesh(mesh.devices.reshape(2, LINES, 2, 4, 4), ("slab", "x", "core", "y", "z"))
    row, col = ("x", "core"), ("y", "z")
    in_specs = (P(row, col, None), P(row, col, None), P(row, col)) + (P(),) * 8
    out_specs = P(row, col, "slab", None, None)
    return jax.shard_map(
        on_device, mesh=fine, in_specs=in_specs, out_specs=out_specs, check_vma=False
    )
```

```python
import jax
import jax.numpy as jnp
from jax import lax
from jax.experimental import pallas as pl
from jax.experimental.pallas import tpu as pltpu
from jax.sharding import Mesh
from jax.sharding import PartitionSpec as P

BF16 = jnp.bfloat16
F32 = jnp.float32
LANES = 128
ROWS = 64
HALF = 16
COLS = 2 * HALF
LOW = 8
CHANNELS = 128
OWN = CHANNELS // 2
POINTS = ROWS * HALF
PITCH = COLS + 8
STEP = HALF + 8
LINES = 4
NEAR = ("z", "x", "y")
FAR = ("z", "x", "y", "slab")


def dot(a, b, ca, cb):
    return lax.dot_general(a, b, (((ca,), (cb,)), ((), ())), preferred_element_type=F32)


def normalize(values):
    average = jnp.mean(values, axis=0, keepdims=True)
    centred = values - average
    inv_std = lax.rsqrt(jnp.mean(centred * centred, axis=0, keepdims=True) + 1e-05)
    return centred * inv_std, inv_std


def mix(a, b):
    low = lax.broadcasted_iota(jnp.int32, a.shape, 1) < ROWS
    first = jnp.where(low, a, pltpu.roll(b, ROWS, 1))
    second = jnp.where(low, pltpu.roll(a, ROWS, 1), b)
    return first, second


def block(m):
    return slice(m * LANES, (m + 1) * LANES)


def load_half(ref, slab_at, scratch):
    start = pl.multiple_of(slab_at * HALF, HALF)
    scratch[...] = ref[:, pl.ds(start, HALF), :].astype(F32).reshape(POINTS, LANES)


def column(scratch, k, width=HALF):
    return scratch[pl.ds(k, ROWS, stride=width), :]


def two_columns(scratch, low):
    return jnp.concatenate([column(scratch, low), column(scratch, low + LOW)], axis=0)


def keep_rows(mask, starts_ref, row_at, col_at):
    wide = jnp.concatenate([mask, mask], axis=1)
    shape = (COLS, LANES)
    lane = lax.broadcasted_iota(jnp.int32, shape, 1)
    row_ids = row_at * ROWS + jnp.where(lane < ROWS, lane, lane - ROWS)
    col_ids = col_at * COLS + lax.broadcasted_iota(jnp.int32, shape, 0)
    row_chain = jnp.zeros(shape, jnp.int32)
    col_chain = jnp.zeros(shape, jnp.int32)
    for at in range(starts_ref.shape[0]):
        start_at = starts_ref[at]
        row_chain = row_chain + (row_ids >= start_at).astype(jnp.int32)
        col_chain = col_chain + (col_ids >= start_at).astype(jnp.int32)
    return jnp.where((row_chain == col_chain) | (wide > 0), 1.0, 0.0)


def halves(a, b):
    return jnp.where(lax.broadcasted_iota(jnp.int32, a.shape, 1) < ROWS, a, b)


def edges_kernel(
    starts_ref, act_ref, mask_ref, gain_ref, bias_ref, w_ref, edges_ref, keep_ref,
    tile, kept, x_all, projected, turned,
):
    slab_at = lax.axis_index("slab")
    row_at = lax.axis_index("x") * 2 + lax.axis_index("core")
    col_at = lax.axis_index("y") * 4 + lax.axis_index("z")
    kept[...] = keep_rows(mask_ref[...], starts_ref, row_at, col_at)
    start = pl.multiple_of(slab_at * HALF, HALF)
    keep_ref[...] = halves(kept[pl.ds(start, LOW), :], kept[pl.ds(start + LOW, LOW), :])
    own = []
    for at in range(2):
        first, second = mix(w_ref[:, block(at)].astype(F32), w_ref[:, block(at + 2)].astype(F32))
        own.append(jnp.where(slab_at == 0, first, second).astype(BF16))
    w_own = jnp.concatenate(own, axis=1)
    values = act_ref[...].astype(F32)
    spare = jnp.zeros((ROWS, PITCH - COLS, LANES), F32)
    tile[...] = jnp.concatenate([values, spare], axis=1).reshape(ROWS * PITCH, LANES)
    gain, bias = (jnp.broadcast_to(ref[...], (LANES, LANES)).T for ref in (gain_ref, bias_ref))
    for k in range(HALF):
        values = jnp.concatenate([column(tile, k, PITCH), column(tile, k + HALF, PITCH)], axis=0)
        normed, _ = normalize(values.T)
        x_all[:, block(k)] = (normed * gain + bias).astype(BF16)
    projected[...] = dot(w_own, x_all[...], 0, 0)
    for k in range(HALF):
        both = jax.nn.sigmoid(projected[0:128, block(k)]) * projected[128:256, block(k)]
        both = both * halves(kept[k : k + 1, :], kept[k + HALF : k + HALF + 1, :])
        turned[pl.ds(k, OWN, stride=PITCH), :] = both[0:OWN, :]
        turned[pl.ds(k + HALF, OWN, stride=PITCH), :] = both[OWN:CHANNELS, :]
    done = turned[...].reshape(OWN, PITCH, LANES)[:, 0:COLS, :]
    edges_ref[...] = done.reshape(OWN * COLS, LANES).astype(BF16)


def ahead_kernel(
    act_ref, grad_ref, keep_ref, w_proj_ref, w_gate_ref, w_out_ref, gain_ref, bias_ref, in_gain_ref, in_bias_ref,
    slope_ref, grad_hat_ref, factor_ref, normed_ref, inv_ref, tall_ref, tile, x_in, projected,
):
    for at, ref in enumerate((in_gain_ref, gain_ref, bias_ref)):
        tall_ref[at] = jnp.broadcast_to(ref[...], (LANES, LANES)).T
    slab_at = lax.axis_index("slab")
    in_bias = jnp.broadcast_to(in_bias_ref[...], (LANES, LANES)).T
    load_half(act_ref, slab_at, tile)
    for low in range(LOW):
        normed, inv = normalize(two_columns(tile, low).T)
        normed_ref[:, block(low)] = normed
        inv_ref[:, block(low)] = inv
        x_in[:, block(low)] = (normed * tall_ref[0] + in_bias).astype(BF16)
    load_half(grad_ref, slab_at, tile)
    gain = tall_ref[1]
    for low in range(LOW):
        here = pl.ds(low * LANES, LANES)
        gate = jax.nn.sigmoid(dot(x_in[:, block(low)], w_gate_ref[...], 0, 0))
        grad_in = two_columns(tile, low)
        slope_ref[here, :] = grad_in * gate * (1.0 - gate)
        mid_in_grad = (grad_in * gate).astype(BF16)
        grad_hat = dot(w_out_ref[...], mid_in_grad, 1, 1) * gain
        grad_hat_ref[pl.ds(low, CHANNELS, stride=LOW), :] = grad_hat - jnp.mean(grad_hat, axis=0, keepdims=True)
    projected[...] = dot(w_proj_ref[...], x_in[...], 0, 0)
    for low in range(LOW):
        keep = keep_ref[low : low + 1, :]
        for side in range(2):
            at = side * 256
            sig = jax.nn.sigmoid(projected[at : at + 128, block(low)])
            value = projected[at + 128 : at + 256, block(low)]
            factor_ref[at : at + 128, block(low)] = (keep * value * sig * (1.0 - sig)).astype(BF16)
            factor_ref[at + 128 : at + 256, block(low)] = (keep * sig).astype(BF16)


def sort_kernel(edges_ref, left_ref, right_ref):
    for m in range(LINES // 2):
        for side, ref in enumerate((left_ref, right_ref)):
            a, b = (
                jnp.concatenate(
                    [
                        edges_ref[pl.ds((z * 16 + x * 4 + y) * COLS + side * HALF, HALF), :].astype(F32)
                        for z in range(LINES)
                        for y in range(LINES)
                    ],
                    axis=0,
                )
                for x in (2 * m, 2 * m + 1)
            )
            first, second = mix(a, b)
            both = jnp.concatenate(
                [first.reshape(16, HALF, LANES), second.reshape(16, HALF, LANES)], axis=1
            )
            ref[:, block(m)] = both.reshape(512, LANES).astype(BF16)


def pieces_of(left_ref, right_ref, put):
    for m in range(LINES // 2):
        tri = dot(right_ref[...], left_ref[:, block(m)], 0, 0)
        tri = tri.reshape(16, HALF, LANES)
        a = tri[:, 0:LOW, :].reshape(LANES, LANES)
        b = tri[:, LOW:HALF, :].reshape(LANES, LANES)
        for x, part in zip((2 * m, 2 * m + 1), mix(a, b)):
            part = part.reshape(LINES, 2, HALF, LANES)
            for z in range(2):
                put((z * 4 + x) * 64, part[:, z].reshape(64, LANES).astype(BF16))


def own_kernel(left_ref, own_ref, out_ref):
    def put(at, rows):
        out_ref[pl.ds(at, 64), :] = rows

    pieces_of(left_ref, own_ref, put)


def other_kernel(left_ref, other_ref, part_ref, out_ref):
    core_at = lax.axis_index("core")
    out_ref[pl.ds(pl.multiple_of(core_at * 512, 512), 512), :] = part_ref[...]
    start = (1 - core_at) * 512

    def put(at, rows):
        out_ref[pl.ds(pl.multiple_of(start + at, 64), 64), :] = rows

    pieces_of(left_ref, other_ref, put)


def middle_kernel(tri_ref, grad_hat_ref, out_ref, hats_ref):
    parts = tri_ref[...].astype(F32).reshape(OWN, 2 * LOW, LANES)
    tri = jnp.concatenate([parts[:, 0:LOW, :], parts[:, LOW : 2 * LOW, :]], axis=0)
    average = jnp.mean(tri, axis=0, keepdims=True)
    centred = tri - average
    inv = lax.rsqrt(jnp.mean(centred * centred, axis=0, keepdims=True) + 1e-05)
    hat = centred * inv
    hats_ref[...] = hat.reshape(CHANNELS * LOW, LANES)
    grad_hat = grad_hat_ref[...].reshape(CHANNELS, LOW, LANES)
    second = jnp.mean(grad_hat * hat, axis=0, keepdims=True)
    done = (grad_hat - hat * second) * inv
    both = jnp.concatenate([done[0:OWN], done[OWN:CHANNELS]], axis=1)
    out_ref[...] = both.astype(BF16).reshape(CHANNELS * LOW, LANES)


def late_kernel(
    hats_ref, slope_ref, w_gate_ref, w_out_ref, tall_ref, own_ref, other_ref, grid_t_ref, out_ref, left_grad_ref
):
    left_grad_ref[...] = dot(own_ref[...], grid_t_ref[0], 1, 0) + dot(other_ref[...], grid_t_ref[1], 1, 0)
    gain, bias = tall_ref[1], tall_ref[2]
    for low in range(LOW):
        hat = hats_ref[pl.ds(low, CHANNELS, stride=LOW), :]
        mid_out = (hat * gain + bias).astype(BF16)
        proj_out = dot(mid_out, w_out_ref[...], 0, 0)
        gate_grad = (slope_ref[pl.ds(low * LANES, LANES), :] * proj_out).astype(BF16)
        out_ref[:, block(low)] = dot(w_gate_ref[...], gate_grad, 1, 1)


def grads_kernel(tri_grad_ref, left_ref, own_ref, other_ref, grid_t):
    core_at = lax.axis_index("core")
    for group, core in enumerate((core_at, 1 - core_at)):
        for m in range(LINES // 2):
            a, b = (
                jnp.concatenate(
                    [
                        tri_grad_ref[
                            pl.ds(pl.multiple_of(core * 512 + (z * 16 + x * 4 + y) * HALF, HALF), HALF), :
                        ].astype(F32)
                        for y in range(LINES)
                        for z in range(2)
                    ],
                    axis=0,
                )
                for x in (2 * m, 2 * m + 1)
            )
            first, second = mix(a, b)
            both = jnp.concatenate(
                [first.reshape(16, LOW, LANES), second.reshape(16, LOW, LANES)], axis=1
            )
            grid_t[group, :, block(m)] = both.reshape(256, LANES).astype(BF16)
    own_ref[...] = dot(left_ref[...], grid_t[0], 1, 1)
    other_ref[...] = dot(left_ref[...], grid_t[1], 1, 1).astype(BF16)


def join_kernel(left_grad_ref, own_ref, other_ref, out_ref):
    for m in range(LINES // 2):
        left_grad = left_grad_ref[:, block(m)]
        right_grad = own_ref[:, block(m)] + other_ref[:, block(m)].astype(F32)
        sides = []
        for grad in (left_grad, right_grad):
            grad = grad.reshape(32, HALF, LANES)
            a = grad[:, 0:LOW, :].reshape(256, LANES)
            b = grad[:, LOW:HALF, :].reshape(256, LANES)
            sides.append([part.reshape(32, LOW, LANES) for part in mix(a, b)])
        for at, x in enumerate((2 * m, 2 * m + 1)):
            both = jnp.concatenate([sides[0][at], sides[1][at]], axis=1)
            both = both.astype(BF16).reshape(512, LANES)
            for z in range(LINES):
                out_ref[pl.ds((z * 4 + x) * LANES, LANES), :] = both[z * LANES : (z + 1) * LANES]


def final_kernel(
    grads_ref, factor_ref, part_ref, normed_ref, inv_ref, w_proj_ref, tall_ref, out_ref,
    grads, proj_grad, result,
):
    got = grads_ref[...].astype(F32).reshape(OWN, 2, HALF, LANES)
    spare = jnp.zeros((OWN, STEP - HALF, LANES), F32)
    for slab in range(2):
        part = jnp.concatenate([got[:, slab], spare], axis=1)
        grads[pl.ds(slab * OWN * STEP, OWN * STEP), :] = part.reshape(OWN * STEP, LANES)
    for low in range(LOW):
        for side in range(2):
            grad = jnp.concatenate(
                [
                    grads[pl.ds(slab * OWN * STEP + side * LOW + low, OWN, stride=STEP), :]
                    for slab in range(2)
                ],
                axis=0,
            )
            for at in (side * 256, side * 256 + 128):
                factor = factor_ref[at : at + 128, block(low)].astype(F32)
                proj_grad[at : at + 128, block(low)] = (grad * factor).astype(BF16)
    gain = tall_ref[0]
    for low in range(LOW):
        x_grad = dot(w_proj_ref[...], proj_grad[:, block(low)], 1, 0) + part_ref[:, block(low)]
        normed = normed_ref[:, block(low)]
        in_hat = x_grad * gain
        first = jnp.mean(in_hat, axis=0, keepdims=True)
        second = jnp.mean(in_hat * normed, axis=0, keepdims=True)
        done = ((in_hat - first - normed * second) * inv_ref[:, block(low)]).T
        result[pl.ds(low, ROWS, stride=STEP), :] = done[0:ROWS, :]
        result[pl.ds(low + LOW, ROWS, stride=STEP), :] = done[ROWS:LANES, :]
    out_ref[...] = result[...].reshape(ROWS, STEP, LANES)[:, 0:HALF, :].astype(BF16)


SMEM = pl.BlockSpec(memory_space=pltpu.SMEM)
VMEM = pl.BlockSpec(memory_space=pltpu.VMEM)


def call(kernel, outs, scratch, args, name, smem=0, cost=None, room=24):
    single = not isinstance(outs, list)
    return pl.pallas_call(
        kernel,
        out_shape=outs,
        in_specs=[SMEM] * smem + [VMEM] * (len(args) - smem),
        out_specs=VMEM if single else [VMEM] * len(outs),
        scratch_shapes=scratch,
        compiler_params=pltpu.CompilerParams(vmem_limit_bytes=room * 1024 * 1024),
        cost_estimate=cost,
        name=name,
    )(*args)


def shape(dims, kind):
    return jax.ShapeDtypeStruct(dims, kind)


def exchange(flat, axes):
    pieces = lax.axis_size(axes)
    cut = flat.reshape(pieces, flat.shape[0] // pieces, LANES)
    return lax.all_to_all(cut, axes, 0, 0, tiled=True).reshape(flat.shape)


def swap(x):
    return lax.ppermute(x, "core", [(0, 1), (1, 0)])


def on_device(
    pair_act, out_grad, pair_mask, chain_starts, in_gain, in_bias, w_proj, w_gate, w_out, mid_gain, mid_bias
):
    in_gain, in_bias, mid_gain, mid_bias = (
        v.reshape(1, LANES) for v in (in_gain, in_bias, mid_gain, mid_bias)
    )
    edge_rows = OWN * COLS
    tri_rows = CHANNELS * LOW
    edges, keep = call(
        edges_kernel,
        [shape((edge_rows, LANES), BF16), shape((LOW, LANES), F32)],
        [
            pltpu.VMEM((ROWS * PITCH, LANES), F32),
            pltpu.VMEM((COLS, LANES), F32),
            pltpu.VMEM((LANES, 2 * POINTS), BF16),
            pltpu.VMEM((256, 2 * POINTS), F32),
            pltpu.VMEM((OWN * PITCH, LANES), F32),
        ],
        (chain_starts, pair_act, pair_mask.T, in_gain, in_bias, w_proj),
        "edges",
        smem=1,
        room=63,
    )
    edges = exchange(edges, NEAR)
    slope, grad_hat, factor, normed, inv, tall = call(
        ahead_kernel,
        [
            shape((POINTS, LANES), F32),
            shape((tri_rows, LANES), F32),
            shape((512, POINTS), BF16),
            shape((LANES, POINTS), F32),
            shape((1, POINTS), F32),
            shape((3, LANES, LANES), F32),
        ],
        [
            pltpu.VMEM((POINTS, LANES), F32),
            pltpu.VMEM((LANES, POINTS), BF16),
            pltpu.VMEM((512, POINTS), F32),
        ],
        (pair_act, out_grad, keep, w_proj, w_gate, w_out, mid_gain, mid_bias, in_gain, in_bias),
        "ahead",
        cost=pl.CostEstimate(flops=300_000_000, bytes_accessed=6_000_000, transcendentals=700_000),
    )
    edges, slope, grad_hat, factor, normed, inv, tall = lax.optimization_barrier(
        (edges, slope, grad_hat, factor, normed, inv, tall)
    )
    left, own = call(
        sort_kernel, [shape((512, 256), BF16), shape((512, 256), BF16)], [], (edges,), "sort"
    )
    other = swap(own)
    part = call(own_kernel, shape((tri_rows // 2, LANES), BF16), [], (left, own), "triangle_own")
    other, part = lax.optimization_barrier((other, part))
    tri = call(
        other_kernel, shape((tri_rows, LANES), BF16), [], (left, other, part), "triangle_other"
    )
    tri = exchange(tri, FAR)
    tri_grad, hats = call(
        middle_kernel,
        [shape((tri_rows, LANES), BF16), shape((tri_rows, LANES), F32)],
        [],
        (tri, grad_hat),
        "middle",
    )
    tri_grad = exchange(tri_grad, FAR)
    own_grad, other_grad, grid_t = call(
        grads_kernel,
        [shape((512, 256), F32), shape((512, 256), BF16), shape((2, 256, 256), BF16)],
        [],
        (tri_grad, left),
        "grads",
    )
    other_grad, hats, grid_t = lax.optimization_barrier((other_grad, hats, grid_t))
    swapped = swap(other_grad)
    part, left_grad = call(
        late_kernel,
        [shape((LANES, POINTS), F32), shape((512, 256), F32)],
        [],
        (hats, slope, w_gate, w_out, tall, own, other, grid_t),
        "late",
        cost=pl.CostEstimate(flops=210_000_000, bytes_accessed=3_000_000, transcendentals=0),
    )
    swapped, part, left_grad = lax.optimization_barrier((swapped, part, left_grad))
    grads = call(
        join_kernel, shape((CHANNELS * HALF, LANES), BF16), [], (left_grad, own_grad, swapped), "join"
    )
    grads = exchange(grads, FAR)
    result = call(
        final_kernel,
        shape((ROWS, HALF, LANES), BF16),
        [
            pltpu.VMEM((CHANNELS * STEP, LANES), F32),
            pltpu.VMEM((512, POINTS), BF16),
            pltpu.VMEM((ROWS * STEP, LANES), F32),
        ],
        (grads, factor, part, normed, inv, w_proj, tall),
        "final",
    )
    return result.reshape(ROWS, 1, 1, HALF, LANES)


def solution(mesh):
    fine = Mesh(mesh.devices.reshape(2, LINES, 2, 4, 4), ("slab", "x", "core", "y", "z"))
    row, col = ("x", "core"), ("y", "z")
    in_specs = (P(row, col, None), P(row, col, None), P(row, col)) + (P(),) * 8
    out_specs = P(row, col, "slab", None, None)
    return jax.shard_map(
        on_device, mesh=fine, in_specs=in_specs, out_specs=out_specs, check_vma=False
    )
```

```python
import jax
import jax.numpy as jnp
from jax import lax
from jax.experimental import pallas as pl
from jax.experimental.pallas import tpu as pltpu
from jax.sharding import Mesh
from jax.sharding import PartitionSpec as P

BF16 = jnp.bfloat16
F32 = jnp.float32
LANES = 128
ROWS = 64
HALF = 16
COLS = 2 * HALF
LOW = 8
CHANNELS = 128
OWN = CHANNELS // 2
POINTS = ROWS * HALF
PITCH = COLS + 8
STEP = HALF + 8
LINES = 4
NEAR = ("z", "x", "y")
FAR = ("z", "x", "y", "slab")


def dot(a, b, ca, cb):
    return lax.dot_general(a, b, (((ca,), (cb,)), ((), ())), preferred_element_type=F32)


def normalize(values):
    average = jnp.mean(values, axis=0, keepdims=True)
    centred = values - average
    inv_std = lax.rsqrt(jnp.mean(centred * centred, axis=0, keepdims=True) + 1e-05)
    return centred * inv_std, inv_std


def mix(a, b):
    low = lax.broadcasted_iota(jnp.int32, a.shape, 1) < ROWS
    first = jnp.where(low, a, pltpu.roll(b, ROWS, 1))
    second = jnp.where(low, pltpu.roll(a, ROWS, 1), b)
    return first, second


def block(m):
    return slice(m * LANES, (m + 1) * LANES)


def load_half(ref, slab_at, scratch):
    start = pl.multiple_of(slab_at * HALF, HALF)
    scratch[...] = ref[:, pl.ds(start, HALF), :].astype(F32).reshape(POINTS, LANES)


def column(scratch, k, width=HALF):
    return scratch[pl.ds(k, ROWS, stride=width), :]


def two_columns(scratch, low):
    return jnp.concatenate([column(scratch, low), column(scratch, low + LOW)], axis=0)


def keep_rows(mask, starts_ref, row_at, col_at):
    wide = jnp.concatenate([mask, mask], axis=1)
    shape = (COLS, LANES)
    lane = lax.broadcasted_iota(jnp.int32, shape, 1)
    row_ids = row_at * ROWS + jnp.where(lane < ROWS, lane, lane - ROWS)
    col_ids = col_at * COLS + lax.broadcasted_iota(jnp.int32, shape, 0)
    row_chain = jnp.zeros(shape, jnp.int32)
    col_chain = jnp.zeros(shape, jnp.int32)
    for at in range(starts_ref.shape[0]):
        start_at = starts_ref[at]
        row_chain = row_chain + (row_ids >= start_at).astype(jnp.int32)
        col_chain = col_chain + (col_ids >= start_at).astype(jnp.int32)
    return jnp.where((row_chain == col_chain) | (wide > 0), 1.0, 0.0)


def halves(a, b):
    return jnp.where(lax.broadcasted_iota(jnp.int32, a.shape, 1) < ROWS, a, b)


def edges_kernel(
    starts_ref, act_ref, mask_ref, gain_ref, bias_ref, w_ref, edges_ref, keep_ref,
    tile, kept, x_all, projected, turned,
):
    slab_at = lax.axis_index("slab")
    row_at = lax.axis_index("x") * 2 + lax.axis_index("core")
    col_at = lax.axis_index("y") * 4 + lax.axis_index("z")
    kept[...] = keep_rows(mask_ref[...], starts_ref, row_at, col_at)
    start = pl.multiple_of(slab_at * HALF, HALF)
    keep_ref[...] = halves(kept[pl.ds(start, LOW), :], kept[pl.ds(start + LOW, LOW), :])
    own = []
    for at in range(2):
        first, second = mix(w_ref[:, block(at)].astype(F32), w_ref[:, block(at + 2)].astype(F32))
        own.append(jnp.where(slab_at == 0, first, second).astype(BF16))
    w_own = jnp.concatenate(own, axis=1)
    values = act_ref[...].astype(F32)
    spare = jnp.zeros((ROWS, PITCH - COLS, LANES), F32)
    tile[...] = jnp.concatenate([values, spare], axis=1).reshape(ROWS * PITCH, LANES)
    gain, bias = (jnp.broadcast_to(ref[...], (LANES, LANES)).T for ref in (gain_ref, bias_ref))
    for k in range(HALF):
        values = jnp.concatenate([column(tile, k, PITCH), column(tile, k + HALF, PITCH)], axis=0)
        normed, _ = normalize(values.T)
        x_all[:, block(k)] = (normed * gain + bias).astype(BF16)
    projected[...] = dot(w_own, x_all[...], 0, 0)
    for k in range(HALF):
        both = jax.nn.sigmoid(projected[0:128, block(k)]) * projected[128:256, block(k)]
        both = both * halves(kept[k : k + 1, :], kept[k + HALF : k + HALF + 1, :])
        turned[pl.ds(k, OWN, stride=PITCH), :] = both[0:OWN, :]
        turned[pl.ds(k + HALF, OWN, stride=PITCH), :] = both[OWN:CHANNELS, :]
    done = turned[...].reshape(OWN, PITCH, LANES)[:, 0:COLS, :]
    edges_ref[...] = done.reshape(OWN * COLS, LANES).astype(BF16)


def ahead_kernel(
    act_ref, grad_ref, keep_ref, w_proj_ref, w_gate_ref, w_out_ref, gain_ref, bias_ref, in_gain_ref, in_bias_ref,
    slope_ref, grad_hat_ref, factor_ref, normed_ref, inv_ref, tall_ref, tile, x_in, projected,
):
    for at, ref in enumerate((in_gain_ref, gain_ref, bias_ref)):
        tall_ref[at] = jnp.broadcast_to(ref[...], (LANES, LANES)).T
    slab_at = lax.axis_index("slab")
    in_bias = jnp.broadcast_to(in_bias_ref[...], (LANES, LANES)).T
    load_half(act_ref, slab_at, tile)
    for low in range(LOW):
        normed, inv = normalize(two_columns(tile, low).T)
        normed_ref[:, block(low)] = normed
        inv_ref[:, block(low)] = inv
        x_in[:, block(low)] = (normed * tall_ref[0] + in_bias).astype(BF16)
    load_half(grad_ref, slab_at, tile)
    gain = tall_ref[1]
    for low in range(LOW):
        here = pl.ds(low * LANES, LANES)
        gate = jax.nn.sigmoid(dot(x_in[:, block(low)], w_gate_ref[...], 0, 0))
        grad_in = two_columns(tile, low)
        slope_ref[here, :] = grad_in * gate * (1.0 - gate)
        mid_in_grad = (grad_in * gate).astype(BF16)
        grad_hat = dot(w_out_ref[...], mid_in_grad, 1, 1) * gain
        grad_hat_ref[pl.ds(low, CHANNELS, stride=LOW), :] = grad_hat - jnp.mean(grad_hat, axis=0, keepdims=True)
    projected[...] = dot(w_proj_ref[...], x_in[...], 0, 0)
    for low in range(LOW):
        keep = keep_ref[low : low + 1, :]
        for side in range(2):
            at = side * 256
            sig = jax.nn.sigmoid(projected[at : at + 128, block(low)])
            value = projected[at + 128 : at + 256, block(low)]
            factor_ref[at : at + 128, block(low)] = (keep * value * sig * (1.0 - sig)).astype(BF16)
            factor_ref[at + 128 : at + 256, block(low)] = (keep * sig).astype(BF16)


def sort(edges_ref, side, ref):
    for m in range(LINES // 2):
        a, b = (
            jnp.concatenate(
                [
                    edges_ref[pl.ds((z * 16 + x * 4 + y) * COLS + side * HALF, HALF), :].astype(F32)
                    for z in range(LINES)
                    for y in range(LINES)
                ],
                axis=0,
            )
            for x in (2 * m, 2 * m + 1)
        )
        first, second = mix(a, b)
        both = jnp.concatenate(
            [first.reshape(16, HALF, LANES), second.reshape(16, HALF, LANES)], axis=1
        )
        ref[:, block(m)] = both.reshape(512, LANES).astype(BF16)


def sort_kernel(edges_ref, right_ref):
    sort(edges_ref, 1, right_ref)


def pieces_of(left_ref, right_ref, put):
    both = dot(right_ref[...], left_ref[...], 0, 0)
    for m in range(LINES // 2):
        tri = both[:, block(m)].reshape(16, HALF, LANES)
        a = tri[:, 0:LOW, :].reshape(LANES, LANES)
        b = tri[:, LOW:HALF, :].reshape(LANES, LANES)
        for x, part in zip((2 * m, 2 * m + 1), mix(a, b)):
            part = part.reshape(LINES, 2, HALF, LANES)
            for z in range(2):
                put((z * 4 + x) * 64, part[:, z].reshape(64, LANES).astype(BF16))


def own_kernel(edges_ref, own_ref, left_ref, out_ref):
    sort(edges_ref, 0, left_ref)

    def put(at, rows):
        out_ref[pl.ds(at, 64), :] = rows

    pieces_of(left_ref, own_ref, put)


def other_kernel(left_ref, other_ref, part_ref, out_ref):
    core_at = lax.axis_index("core")
    out_ref[pl.ds(pl.multiple_of(core_at * 512, 512), 512), :] = part_ref[...]
    start = (1 - core_at) * 512

    def put(at, rows):
        out_ref[pl.ds(pl.multiple_of(start + at, 64), 64), :] = rows

    pieces_of(left_ref, other_ref, put)


def middle_kernel(tri_ref, grad_hat_ref, out_ref, hats_ref):
    parts = tri_ref[...].astype(F32).reshape(OWN, 2 * LOW, LANES)
    tri = jnp.concatenate([parts[:, 0:LOW, :], parts[:, LOW : 2 * LOW, :]], axis=0)
    average = jnp.mean(tri, axis=0, keepdims=True)
    centred = tri - average
    inv = lax.rsqrt(jnp.mean(centred * centred, axis=0, keepdims=True) + 1e-05)
    hat = centred * inv
    hats_ref[...] = hat.reshape(CHANNELS * LOW, LANES)
    grad_hat = grad_hat_ref[...].reshape(CHANNELS, LOW, LANES)
    second = jnp.mean(grad_hat * hat, axis=0, keepdims=True)
    done = (grad_hat - hat * second) * inv
    both = jnp.concatenate([done[0:OWN], done[OWN:CHANNELS]], axis=1)
    out_ref[...] = both.astype(BF16).reshape(CHANNELS * LOW, LANES)


def late_kernel(
    hats_ref, slope_ref, w_gate_ref, w_out_ref, tall_ref, own_ref, other_ref, grid_t_ref, out_ref, left_grad_ref
):
    left_grad_ref[...] = dot(own_ref[...], grid_t_ref[0], 1, 0) + dot(other_ref[...], grid_t_ref[1], 1, 0)
    gain, bias = tall_ref[1], tall_ref[2]
    for low in range(0, LOW, 2):
        hats = [hats_ref[pl.ds(low + at, CHANNELS, stride=LOW), :] for at in range(2)]
        mid_out = jnp.concatenate([(hat * gain + bias).astype(BF16) for hat in hats], axis=1)
        proj_out = dot(mid_out, w_out_ref[...], 0, 0)
        gate_grad = (slope_ref[pl.ds(low * LANES, 2 * LANES), :] * proj_out).astype(BF16)
        out_ref[:, low * LANES : (low + 2) * LANES] = dot(w_gate_ref[...], gate_grad, 1, 1)


def grads_kernel(tri_grad_ref, left_ref, own_ref, other_ref, grid_t):
    core_at = lax.axis_index("core")
    for group, core in enumerate((core_at, 1 - core_at)):
        for m in range(LINES // 2):
            a, b = (
                jnp.concatenate(
                    [
                        tri_grad_ref[
                            pl.ds(pl.multiple_of(core * 512 + (z * 16 + x * 4 + y) * HALF, HALF), HALF), :
                        ].astype(F32)
                        for y in range(LINES)
                        for z in range(2)
                    ],
                    axis=0,
                )
                for x in (2 * m, 2 * m + 1)
            )
            first, second = mix(a, b)
            both = jnp.concatenate(
                [first.reshape(16, LOW, LANES), second.reshape(16, LOW, LANES)], axis=1
            )
            grid_t[group, :, block(m)] = both.reshape(256, LANES).astype(BF16)
    own_ref[...] = dot(left_ref[...], grid_t[0], 1, 1)
    other_ref[...] = dot(left_ref[...], grid_t[1], 1, 1).astype(BF16)


def join_kernel(left_grad_ref, own_ref, other_ref, out_ref):
    for m in range(LINES // 2):
        left_grad = left_grad_ref[:, block(m)]
        right_grad = own_ref[:, block(m)] + other_ref[:, block(m)].astype(F32)
        sides = []
        for grad in (left_grad, right_grad):
            grad = grad.reshape(32, HALF, LANES)
            a = grad[:, 0:LOW, :].reshape(256, LANES)
            b = grad[:, LOW:HALF, :].reshape(256, LANES)
            sides.append([part.reshape(32, LOW, LANES) for part in mix(a, b)])
        for at, x in enumerate((2 * m, 2 * m + 1)):
            both = jnp.concatenate([sides[0][at], sides[1][at]], axis=1)
            both = both.astype(BF16).reshape(512, LANES)
            for z in range(LINES):
                out_ref[pl.ds((z * 4 + x) * LANES, LANES), :] = both[z * LANES : (z + 1) * LANES]


def final_kernel(
    grads_ref, factor_ref, part_ref, normed_ref, inv_ref, w_proj_ref, tall_ref, out_ref,
    grads, proj_grad, result,
):
    got = grads_ref[...].astype(F32).reshape(OWN, 2, HALF, LANES)
    spare = jnp.zeros((OWN, STEP - HALF, LANES), F32)
    for slab in range(2):
        part = jnp.concatenate([got[:, slab], spare], axis=1)
        grads[pl.ds(slab * OWN * STEP, OWN * STEP), :] = part.reshape(OWN * STEP, LANES)
    for low in range(LOW):
        for side in range(2):
            grad = jnp.concatenate(
                [
                    grads[pl.ds(slab * OWN * STEP + side * LOW + low, OWN, stride=STEP), :]
                    for slab in range(2)
                ],
                axis=0,
            )
            for at in (side * 256, side * 256 + 128):
                factor = factor_ref[at : at + 128, block(low)].astype(F32)
                proj_grad[at : at + 128, block(low)] = (grad * factor).astype(BF16)
    gain = tall_ref[0]
    for low in range(LOW):
        if low % 2 == 0:
            pair = dot(w_proj_ref[...], proj_grad[:, low * LANES : (low + 2) * LANES], 1, 0)
        x_grad = pair[:, block(low % 2)] + part_ref[:, block(low)]
        normed = normed_ref[:, block(low)]
        in_hat = x_grad * gain
        first = jnp.mean(in_hat, axis=0, keepdims=True)
        second = jnp.mean(in_hat * normed, axis=0, keepdims=True)
        done = ((in_hat - first - normed * second) * inv_ref[:, block(low)]).T
        result[pl.ds(low, ROWS, stride=STEP), :] = done[0:ROWS, :]
        result[pl.ds(low + LOW, ROWS, stride=STEP), :] = done[ROWS:LANES, :]
    out_ref[...] = result[...].reshape(ROWS, STEP, LANES)[:, 0:HALF, :].astype(BF16)


SMEM = pl.BlockSpec(memory_space=pltpu.SMEM)
VMEM = pl.BlockSpec(memory_space=pltpu.VMEM)


def call(kernel, outs, scratch, args, name, smem=0, cost=None, room=24):
    single = not isinstance(outs, list)
    return pl.pallas_call(
        kernel,
        out_shape=outs,
        in_specs=[SMEM] * smem + [VMEM] * (len(args) - smem),
        out_specs=VMEM if single else [VMEM] * len(outs),
        scratch_shapes=scratch,
        compiler_params=pltpu.CompilerParams(vmem_limit_bytes=room * 1024 * 1024),
        cost_estimate=cost,
        name=name,
    )(*args)


def shape(dims, kind):
    return jax.ShapeDtypeStruct(dims, kind)


def exchange(flat, axes):
    pieces = lax.axis_size(axes)
    cut = flat.reshape(pieces, flat.shape[0] // pieces, LANES)
    return lax.all_to_all(cut, axes, 0, 0, tiled=True).reshape(flat.shape)


def swap(x):
    return lax.ppermute(x, "core", [(0, 1), (1, 0)])


def on_device(
    pair_act, out_grad, pair_mask, chain_starts, in_gain, in_bias, w_proj, w_gate, w_out, mid_gain, mid_bias
):
    in_gain, in_bias, mid_gain, mid_bias = (
        v.reshape(1, LANES) for v in (in_gain, in_bias, mid_gain, mid_bias)
    )
    edge_rows = OWN * COLS
    tri_rows = CHANNELS * LOW
    edges, keep = call(
        edges_kernel,
        [shape((edge_rows, LANES), BF16), shape((LOW, LANES), F32)],
        [
            pltpu.VMEM((ROWS * PITCH, LANES), F32),
            pltpu.VMEM((COLS, LANES), F32),
            pltpu.VMEM((LANES, 2 * POINTS), BF16),
            pltpu.VMEM((256, 2 * POINTS), F32),
            pltpu.VMEM((OWN * PITCH, LANES), F32),
        ],
        (chain_starts, pair_act, pair_mask.T, in_gain, in_bias, w_proj),
        "edges",
        smem=1,
        room=63,
    )
    edges = exchange(edges, NEAR)
    slope, grad_hat, factor, normed, inv, tall = call(
        ahead_kernel,
        [
            shape((POINTS, LANES), F32),
            shape((tri_rows, LANES), F32),
            shape((512, POINTS), BF16),
            shape((LANES, POINTS), F32),
            shape((1, POINTS), F32),
            shape((3, LANES, LANES), F32),
        ],
        [
            pltpu.VMEM((POINTS, LANES), F32),
            pltpu.VMEM((LANES, POINTS), BF16),
            pltpu.VMEM((512, POINTS), F32),
        ],
        (pair_act, out_grad, keep, w_proj, w_gate, w_out, mid_gain, mid_bias, in_gain, in_bias),
        "ahead",
        cost=pl.CostEstimate(flops=300_000_000, bytes_accessed=6_000_000, transcendentals=700_000),
    )
    edges, slope, grad_hat, factor, normed, inv, tall = lax.optimization_barrier(
        (edges, slope, grad_hat, factor, normed, inv, tall)
    )
    own = call(sort_kernel, shape((512, 256), BF16), [], (edges,), "sort")
    other = swap(own)
    left, part = call(
        own_kernel,
        [shape((512, 256), BF16), shape((tri_rows // 2, LANES), BF16)],
        [],
        (edges, own),
        "triangle_own",
    )
    other, left, part = lax.optimization_barrier((other, left, part))
    tri = call(
        other_kernel, shape((tri_rows, LANES), BF16), [], (left, other, part), "triangle_other"
    )
    tri = exchange(tri, FAR)
    tri_grad, hats = call(
        middle_kernel,
        [shape((tri_rows, LANES), BF16), shape((tri_rows, LANES), F32)],
        [],
        (tri, grad_hat),
        "middle",
    )
    tri_grad = exchange(tri_grad, FAR)
    own_grad, other_grad, grid_t = call(
        grads_kernel,
        [shape((512, 256), F32), shape((512, 256), BF16), shape((2, 256, 256), BF16)],
        [],
        (tri_grad, left),
        "grads",
    )
    other_grad, hats, grid_t = lax.optimization_barrier((other_grad, hats, grid_t))
    swapped = swap(other_grad)
    part, left_grad = call(
        late_kernel,
        [shape((LANES, POINTS), F32), shape((512, 256), F32)],
        [],
        (hats, slope, w_gate, w_out, tall, own, other, grid_t),
        "late",
        cost=pl.CostEstimate(flops=210_000_000, bytes_accessed=3_000_000, transcendentals=0),
    )
    swapped, part, left_grad = lax.optimization_barrier((swapped, part, left_grad))
    grads = call(
        join_kernel, shape((CHANNELS * HALF, LANES), BF16), [], (left_grad, own_grad, swapped), "join"
    )
    grads = exchange(grads, FAR)
    result = call(
        final_kernel,
        shape((ROWS, HALF, LANES), BF16),
        [
            pltpu.VMEM((CHANNELS * STEP, LANES), F32),
            pltpu.VMEM((512, POINTS), BF16),
            pltpu.VMEM((ROWS * STEP, LANES), F32),
        ],
        (grads, factor, part, normed, inv, w_proj, tall),
        "final",
    )
    return result.reshape(ROWS, 1, 1, HALF, LANES)


def solution(mesh):
    fine = Mesh(mesh.devices.reshape(2, LINES, 2, 4, 4), ("slab", "x", "core", "y", "z"))
    row, col = ("x", "core"), ("y", "z")
    in_specs = (P(row, col, None), P(row, col, None), P(row, col)) + (P(),) * 8
    out_specs = P(row, col, "slab", None, None)
    return jax.shard_map(
        on_device, mesh=fine, in_specs=in_specs, out_specs=out_specs, check_vma=False
    )
```

```python
import jax
import jax.numpy as jnp
from jax import lax
from jax.experimental import pallas as pl
from jax.experimental.pallas import tpu as pltpu
from jax.sharding import Mesh
from jax.sharding import PartitionSpec as P

BF16 = jnp.bfloat16
F32 = jnp.float32
LANES = 128
ROWS = 64
HALF = 16
COLS = 2 * HALF
LOW = 8
CHANNELS = 128
OWN = CHANNELS // 2
POINTS = ROWS * HALF
PITCH = COLS + 8
STEP = HALF + 8
LINES = 4
NEAR = ("z", "x", "y")
FAR = ("z", "x", "y", "slab")


def dot(a, b, ca, cb):
    return lax.dot_general(a, b, (((ca,), (cb,)), ((), ())), preferred_element_type=F32)


def normalize(values):
    average = jnp.mean(values, axis=0, keepdims=True)
    centred = values - average
    inv_std = lax.rsqrt(jnp.mean(centred * centred, axis=0, keepdims=True) + 1e-05)
    return centred * inv_std, inv_std


def mix(a, b):
    low = lax.broadcasted_iota(jnp.int32, a.shape, 1) < ROWS
    first = jnp.where(low, a, pltpu.roll(b, ROWS, 1))
    second = jnp.where(low, pltpu.roll(a, ROWS, 1), b)
    return first, second


def block(m):
    return slice(m * LANES, (m + 1) * LANES)


def load_half(ref, slab_at, scratch):
    start = pl.multiple_of(slab_at * HALF, HALF)
    scratch[...] = ref[:, pl.ds(start, HALF), :].astype(F32).reshape(POINTS, LANES)


def column(scratch, k, width=HALF):
    return scratch[pl.ds(k, ROWS, stride=width), :]


def two_columns(scratch, low):
    return jnp.concatenate([column(scratch, low), column(scratch, low + LOW)], axis=0)


def keep_rows(mask, starts_ref, row_at, col_at):
    wide = jnp.concatenate([mask, mask], axis=1)
    shape = (COLS, LANES)
    lane = lax.broadcasted_iota(jnp.int32, shape, 1)
    row_ids = row_at * ROWS + jnp.where(lane < ROWS, lane, lane - ROWS)
    col_ids = col_at * COLS + lax.broadcasted_iota(jnp.int32, shape, 0)
    row_chain = jnp.zeros(shape, jnp.int32)
    col_chain = jnp.zeros(shape, jnp.int32)
    for at in range(starts_ref.shape[0]):
        start_at = starts_ref[at]
        row_chain = row_chain + (row_ids >= start_at).astype(jnp.int32)
        col_chain = col_chain + (col_ids >= start_at).astype(jnp.int32)
    return jnp.where((row_chain == col_chain) | (wide > 0), 1.0, 0.0)


def halves(a, b):
    return jnp.where(lax.broadcasted_iota(jnp.int32, a.shape, 1) < ROWS, a, b)


def edges_kernel(
    starts_ref, act_ref, mask_ref, gain_ref, bias_ref, w_ref, edges_ref, keep_ref,
    tile, kept, x_all, projected, turned,
):
    slab_at = lax.axis_index("slab")
    row_at = lax.axis_index("x") * 2 + lax.axis_index("core")
    col_at = lax.axis_index("y") * 4 + lax.axis_index("z")
    kept[...] = keep_rows(mask_ref[...], starts_ref, row_at, col_at)
    start = pl.multiple_of(slab_at * HALF, HALF)
    keep_ref[...] = halves(kept[pl.ds(start, LOW), :], kept[pl.ds(start + LOW, LOW), :])
    own = []
    for at in range(2):
        first, second = mix(w_ref[:, block(at)].astype(F32), w_ref[:, block(at + 2)].astype(F32))
        own.append(jnp.where(slab_at == 0, first, second).astype(BF16))
    w_own = jnp.concatenate(own, axis=1)
    values = act_ref[...].astype(F32)
    spare = jnp.zeros((ROWS, PITCH - COLS, LANES), F32)
    tile[...] = jnp.concatenate([values, spare], axis=1).reshape(ROWS * PITCH, LANES)
    gain, bias = (jnp.broadcast_to(ref[...], (LANES, LANES)).T for ref in (gain_ref, bias_ref))
    for k in range(HALF):
        values = jnp.concatenate([column(tile, k, PITCH), column(tile, k + HALF, PITCH)], axis=0)
        normed, _ = normalize(values.T)
        x_all[:, block(k)] = (normed * gain + bias).astype(BF16)
    projected[...] = dot(w_own, x_all[...], 0, 0)
    for k in range(HALF):
        both = jax.nn.sigmoid(projected[0:128, block(k)]) * projected[128:256, block(k)]
        both = both * halves(kept[k : k + 1, :], kept[k + HALF : k + HALF + 1, :])
        turned[pl.ds(k, OWN, stride=PITCH), :] = both[0:OWN, :]
        turned[pl.ds(k + HALF, OWN, stride=PITCH), :] = both[OWN:CHANNELS, :]
    done = turned[...].reshape(OWN, PITCH, LANES)[:, 0:COLS, :]
    edges_ref[...] = done.reshape(OWN * COLS, LANES).astype(BF16)


def ahead_kernel(
    act_ref, grad_ref, keep_ref, w_proj_ref, w_gate_ref, w_out_ref, gain_ref, bias_ref, in_gain_ref, in_bias_ref,
    slope_ref, grad_hat_ref, factor_ref, normed_ref, inv_ref, tall_ref, tile, x_in, projected,
):
    for at, ref in enumerate((in_gain_ref, gain_ref, bias_ref)):
        tall_ref[at] = jnp.broadcast_to(ref[...], (LANES, LANES)).T
    slab_at = lax.axis_index("slab")
    in_bias = jnp.broadcast_to(in_bias_ref[...], (LANES, LANES)).T
    load_half(act_ref, slab_at, tile)
    for low in range(LOW):
        normed, inv = normalize(two_columns(tile, low).T)
        normed_ref[:, block(low)] = normed
        inv_ref[:, block(low)] = inv
        x_in[:, block(low)] = (normed * tall_ref[0] + in_bias).astype(BF16)
    load_half(grad_ref, slab_at, tile)
    gain = tall_ref[1]
    for low in range(LOW):
        here = pl.ds(low * LANES, LANES)
        gate = jax.nn.sigmoid(dot(x_in[:, block(low)], w_gate_ref[...], 0, 0))
        grad_in = two_columns(tile, low)
        slope_ref[here, :] = grad_in * gate * (1.0 - gate)
        mid_in_grad = (grad_in * gate).astype(BF16)
        grad_hat = dot(w_out_ref[...], mid_in_grad, 1, 1) * gain
        grad_hat_ref[pl.ds(low, CHANNELS, stride=LOW), :] = grad_hat - jnp.mean(grad_hat, axis=0, keepdims=True)
    projected[...] = dot(w_proj_ref[...], x_in[...], 0, 0)
    for low in range(LOW):
        keep = keep_ref[low : low + 1, :]
        for side in range(2):
            at = side * 256
            sig = jax.nn.sigmoid(projected[at : at + 128, block(low)])
            value = projected[at + 128 : at + 256, block(low)]
            factor_ref[at : at + 128, block(low)] = (keep * value * sig * (1.0 - sig)).astype(BF16)
            factor_ref[at + 128 : at + 256, block(low)] = (keep * sig).astype(BF16)


def sort(edges_ref, side, ref):
    for m in range(LINES // 2):
        a, b = (
            jnp.concatenate(
                [
                    edges_ref[pl.ds((z * 16 + x * 4 + y) * COLS + side * HALF, HALF), :].astype(F32)
                    for z in range(LINES)
                    for y in range(LINES)
                ],
                axis=0,
            )
            for x in (2 * m, 2 * m + 1)
        )
        first, second = mix(a, b)
        both = jnp.concatenate(
            [first.reshape(16, HALF, LANES), second.reshape(16, HALF, LANES)], axis=1
        )
        ref[:, block(m)] = both.reshape(512, LANES).astype(BF16)


def sort_kernel(edges_ref, right_ref):
    sort(edges_ref, 1, right_ref)


def pieces_of(left_ref, right_ref, put):
    both = dot(right_ref[...], left_ref[...], 0, 0)
    for m in range(LINES // 2):
        tri = both[:, block(m)].reshape(16, HALF, LANES)
        a = tri[:, 0:LOW, :].reshape(LANES, LANES)
        b = tri[:, LOW:HALF, :].reshape(LANES, LANES)
        for x, part in zip((2 * m, 2 * m + 1), mix(a, b)):
            part = part.reshape(LINES, 2, HALF, LANES)
            for z in range(2):
                put((z * 4 + x) * 64, part[:, z].reshape(64, LANES).astype(BF16))


def own_kernel(edges_ref, own_ref, left_ref, out_ref):
    sort(edges_ref, 0, left_ref)

    def put(at, rows):
        out_ref[pl.ds(at, 64), :] = rows

    pieces_of(left_ref, own_ref, put)


def other_kernel(left_ref, other_ref, part_ref, out_ref):
    core_at = lax.axis_index("core")
    out_ref[pl.ds(pl.multiple_of(core_at * 512, 512), 512), :] = part_ref[...]
    start = (1 - core_at) * 512

    def put(at, rows):
        out_ref[pl.ds(pl.multiple_of(start + at, 64), 64), :] = rows

    pieces_of(left_ref, other_ref, put)


def middle_kernel(tri_ref, grad_hat_ref, out_ref, hats_ref):
    parts = tri_ref[...].astype(F32).reshape(OWN, 2 * LOW, LANES)
    tri = jnp.concatenate([parts[:, 0:LOW, :], parts[:, LOW : 2 * LOW, :]], axis=0)
    average = jnp.mean(tri, axis=0, keepdims=True)
    centred = tri - average
    inv = lax.rsqrt(jnp.mean(centred * centred, axis=0, keepdims=True) + 1e-05)
    hat = centred * inv
    hats_ref[...] = hat.reshape(CHANNELS * LOW, LANES)
    grad_hat = grad_hat_ref[...].reshape(CHANNELS, LOW, LANES)
    second = jnp.mean(grad_hat * hat, axis=0, keepdims=True)
    done = (grad_hat - hat * second) * inv
    both = jnp.concatenate([done[0:OWN], done[OWN:CHANNELS]], axis=1)
    out_ref[...] = both.astype(BF16).reshape(CHANNELS * LOW, LANES)


def two_rows(grad):
    grad = grad.reshape(32, HALF, LANES)
    return mix(grad[:, 0:LOW, :].reshape(256, LANES), grad[:, LOW:HALF, :].reshape(256, LANES))


def late_kernel(
    hats_ref, slope_ref, w_gate_ref, w_out_ref, tall_ref, left_ref, own_ref, other_ref, grid_t_ref,
    out_ref, left_grad_ref, right_grad_ref,
):
    right_grad_ref[...] = dot(left_ref[...], grid_t_ref[0], 1, 1)
    left_grad = dot(own_ref[...], grid_t_ref[0], 1, 0) + dot(other_ref[...], grid_t_ref[1], 1, 0)
    for m in range(LINES // 2):
        left_grad_ref[2 * m], left_grad_ref[2 * m + 1] = two_rows(left_grad[:, block(m)])
    gain, bias = tall_ref[1], tall_ref[2]
    for low in range(0, LOW, 2):
        hats = [hats_ref[pl.ds(low + at, CHANNELS, stride=LOW), :] for at in range(2)]
        mid_out = jnp.concatenate([(hat * gain + bias).astype(BF16) for hat in hats], axis=1)
        proj_out = dot(mid_out, w_out_ref[...], 0, 0)
        gate_grad = (slope_ref[pl.ds(low * LANES, 2 * LANES), :] * proj_out).astype(BF16)
        out_ref[:, low * LANES : (low + 2) * LANES] = dot(w_gate_ref[...], gate_grad, 1, 1)


def grads_kernel(tri_grad_ref, left_ref, other_ref, grid_t):
    core_at = lax.axis_index("core")
    for group, core in enumerate((core_at, 1 - core_at)):
        for m in range(LINES // 2):
            a, b = (
                jnp.concatenate(
                    [
                        tri_grad_ref[
                            pl.ds(pl.multiple_of(core * 512 + (z * 16 + x * 4 + y) * HALF, HALF), HALF), :
                        ].astype(F32)
                        for y in range(LINES)
                        for z in range(2)
                    ],
                    axis=0,
                )
                for x in (2 * m, 2 * m + 1)
            )
            first, second = mix(a, b)
            both = jnp.concatenate(
                [first.reshape(16, LOW, LANES), second.reshape(16, LOW, LANES)], axis=1
            )
            grid_t[group, :, block(m)] = both.reshape(256, LANES).astype(BF16)
    other_ref[...] = dot(left_ref[...], grid_t[1], 1, 1).astype(BF16)


def join_kernel(left_grad_ref, own_ref, other_ref, out_ref):
    for m in range(LINES // 2):
        right_grad = own_ref[:, block(m)] + other_ref[:, block(m)].astype(F32)
        for x, part in zip((2 * m, 2 * m + 1), two_rows(right_grad)):
            left_grad = left_grad_ref[x].reshape(32, LOW, LANES)
            both = jnp.concatenate([left_grad, part.reshape(32, LOW, LANES)], axis=1)
            both = both.astype(BF16).reshape(512, LANES)
            for z in range(LINES):
                out_ref[pl.ds((z * 4 + x) * LANES, LANES), :] = both[z * LANES : (z + 1) * LANES]


def final_kernel(
    grads_ref, factor_ref, part_ref, normed_ref, inv_ref, w_proj_ref, tall_ref, out_ref,
    grads, proj_grad, result,
):
    got = grads_ref[...].astype(F32).reshape(OWN, 2, HALF, LANES)
    spare = jnp.zeros((OWN, STEP - HALF, LANES), F32)
    for slab in range(2):
        part = jnp.concatenate([got[:, slab], spare], axis=1)
        grads[pl.ds(slab * OWN * STEP, OWN * STEP), :] = part.reshape(OWN * STEP, LANES)
    for low in range(LOW):
        for side in range(2):
            grad = jnp.concatenate(
                [
                    grads[pl.ds(slab * OWN * STEP + side * LOW + low, OWN, stride=STEP), :]
                    for slab in range(2)
                ],
                axis=0,
            )
            for at in (side * 256, side * 256 + 128):
                factor = factor_ref[at : at + 128, block(low)].astype(F32)
                proj_grad[at : at + 128, block(low)] = (grad * factor).astype(BF16)
    gain = tall_ref[0]
    for low in range(LOW):
        if low % 2 == 0:
            pair = dot(w_proj_ref[...], proj_grad[:, low * LANES : (low + 2) * LANES], 1, 0)
        x_grad = pair[:, block(low % 2)] + part_ref[:, block(low)]
        normed = normed_ref[:, block(low)]
        in_hat = x_grad * gain
        first = jnp.mean(in_hat, axis=0, keepdims=True)
        second = jnp.mean(in_hat * normed, axis=0, keepdims=True)
        done = ((in_hat - first - normed * second) * inv_ref[:, block(low)]).T
        result[pl.ds(low, ROWS, stride=STEP), :] = done[0:ROWS, :]
        result[pl.ds(low + LOW, ROWS, stride=STEP), :] = done[ROWS:LANES, :]
    out_ref[...] = result[...].reshape(ROWS, STEP, LANES)[:, 0:HALF, :].astype(BF16)


SMEM = pl.BlockSpec(memory_space=pltpu.SMEM)
VMEM = pl.BlockSpec(memory_space=pltpu.VMEM)


def call(kernel, outs, scratch, args, name, smem=0, cost=None, room=24):
    single = not isinstance(outs, list)
    return pl.pallas_call(
        kernel,
        out_shape=outs,
        in_specs=[SMEM] * smem + [VMEM] * (len(args) - smem),
        out_specs=VMEM if single else [VMEM] * len(outs),
        scratch_shapes=scratch,
        compiler_params=pltpu.CompilerParams(vmem_limit_bytes=room * 1024 * 1024),
        cost_estimate=cost,
        name=name,
    )(*args)


def shape(dims, kind):
    return jax.ShapeDtypeStruct(dims, kind)


def exchange(flat, axes):
    pieces = lax.axis_size(axes)
    cut = flat.reshape(pieces, flat.shape[0] // pieces, LANES)
    return lax.all_to_all(cut, axes, 0, 0, tiled=True).reshape(flat.shape)


def swap(x):
    return lax.ppermute(x, "core", [(0, 1), (1, 0)])


def on_device(
    pair_act, out_grad, pair_mask, chain_starts, in_gain, in_bias, w_proj, w_gate, w_out, mid_gain, mid_bias
):
    in_gain, in_bias, mid_gain, mid_bias = (
        v.reshape(1, LANES) for v in (in_gain, in_bias, mid_gain, mid_bias)
    )
    edge_rows = OWN * COLS
    tri_rows = CHANNELS * LOW
    edges, keep = call(
        edges_kernel,
        [shape((edge_rows, LANES), BF16), shape((LOW, LANES), F32)],
        [
            pltpu.VMEM((ROWS * PITCH, LANES), F32),
            pltpu.VMEM((COLS, LANES), F32),
            pltpu.VMEM((LANES, 2 * POINTS), BF16),
            pltpu.VMEM((256, 2 * POINTS), F32),
            pltpu.VMEM((OWN * PITCH, LANES), F32),
        ],
        (chain_starts, pair_act, pair_mask.T, in_gain, in_bias, w_proj),
        "edges",
        smem=1,
        room=63,
    )
    edges = exchange(edges, NEAR)
    slope, grad_hat, factor, normed, inv, tall = call(
        ahead_kernel,
        [
            shape((POINTS, LANES), F32),
            shape((tri_rows, LANES), F32),
            shape((512, POINTS), BF16),
            shape((LANES, POINTS), F32),
            shape((1, POINTS), F32),
            shape((3, LANES, LANES), F32),
        ],
        [
            pltpu.VMEM((POINTS, LANES), F32),
            pltpu.VMEM((LANES, POINTS), BF16),
            pltpu.VMEM((512, POINTS), F32),
        ],
        (pair_act, out_grad, keep, w_proj, w_gate, w_out, mid_gain, mid_bias, in_gain, in_bias),
        "ahead",
        cost=pl.CostEstimate(flops=300_000_000, bytes_accessed=6_000_000, transcendentals=700_000),
    )
    edges, slope, grad_hat, factor, normed, inv, tall = lax.optimization_barrier(
        (edges, slope, grad_hat, factor, normed, inv, tall)
    )
    own = call(sort_kernel, shape((512, 256), BF16), [], (edges,), "sort")
    other = swap(own)
    left, part = call(
        own_kernel,
        [shape((512, 256), BF16), shape((tri_rows // 2, LANES), BF16)],
        [],
        (edges, own),
        "triangle_own",
    )
    other, left, part = lax.optimization_barrier((other, left, part))
    tri = call(
        other_kernel, shape((tri_rows, LANES), BF16), [], (left, other, part), "triangle_other"
    )
    tri = exchange(tri, FAR)
    tri_grad, hats = call(
        middle_kernel,
        [shape((tri_rows, LANES), BF16), shape((tri_rows, LANES), F32)],
        [],
        (tri, grad_hat),
        "middle",
    )
    tri_grad = exchange(tri_grad, FAR)
    other_grad, grid_t = call(
        grads_kernel,
        [shape((512, 256), BF16), shape((2, 256, 256), BF16)],
        [],
        (tri_grad, left),
        "grads",
    )
    other_grad, hats, grid_t = lax.optimization_barrier((other_grad, hats, grid_t))
    swapped = swap(other_grad)
    part, left_grad, own_grad = call(
        late_kernel,
        [shape((LANES, POINTS), F32), shape((LINES, 256, LANES), F32), shape((512, 256), F32)],
        [],
        (hats, slope, w_gate, w_out, tall, left, own, other, grid_t),
        "late",
        cost=pl.CostEstimate(flops=210_000_000, bytes_accessed=3_000_000, transcendentals=0),
    )
    swapped, part, left_grad, own_grad = lax.optimization_barrier((swapped, part, left_grad, own_grad))
    grads = call(
        join_kernel, shape((CHANNELS * HALF, LANES), BF16), [], (left_grad, own_grad, swapped), "join"
    )
    grads = exchange(grads, FAR)
    result = call(
        final_kernel,
        shape((ROWS, HALF, LANES), BF16),
        [
            pltpu.VMEM((CHANNELS * STEP, LANES), F32),
            pltpu.VMEM((512, POINTS), BF16),
            pltpu.VMEM((ROWS * STEP, LANES), F32),
        ],
        (grads, factor, part, normed, inv, w_proj, tall),
        "final",
    )
    return result.reshape(ROWS, 1, 1, HALF, LANES)


def solution(mesh):
    fine = Mesh(mesh.devices.reshape(2, LINES, 2, 4, 4), ("slab", "x", "core", "y", "z"))
    row, col = ("x", "core"), ("y", "z")
    in_specs = (P(row, col, None), P(row, col, None), P(row, col)) + (P(),) * 8
    out_specs = P(row, col, "slab", None, None)
    return jax.shard_map(
        on_device, mesh=fine, in_specs=in_specs, out_specs=out_specs, check_vma=False
    )
```

```python
import jax
import jax.numpy as jnp
from jax import lax
from jax.experimental import pallas as pl
from jax.experimental.pallas import tpu as pltpu
from jax.sharding import Mesh
from jax.sharding import PartitionSpec as P

BF16 = jnp.bfloat16
F32 = jnp.float32
LANES = 128
ROWS = 64
HALF = 16
COLS = 2 * HALF
LOW = 8
CHANNELS = 128
OWN = CHANNELS // 2
POINTS = ROWS * HALF
PITCH = COLS + 8
STEP = HALF + 8
LINES = 4
NEAR = ("z", "x", "y")
FAR = ("z", "x", "y", "slab")


def dot(a, b, ca, cb):
    return lax.dot_general(a, b, (((ca,), (cb,)), ((), ())), preferred_element_type=F32)


def normalize(values):
    average = jnp.mean(values, axis=0, keepdims=True)
    centred = values - average
    inv_std = lax.rsqrt(jnp.mean(centred * centred, axis=0, keepdims=True) + 1e-05)
    return centred * inv_std, inv_std


def mix(a, b):
    low = lax.broadcasted_iota(jnp.int32, a.shape, 1) < ROWS
    first = jnp.where(low, a, pltpu.roll(b, ROWS, 1))
    second = jnp.where(low, pltpu.roll(a, ROWS, 1), b)
    return first, second


def block(m):
    return slice(m * LANES, (m + 1) * LANES)


def load_half(ref, slab_at, scratch):
    start = pl.multiple_of(slab_at * HALF, HALF)
    scratch[...] = ref[:, pl.ds(start, HALF), :].astype(F32).reshape(POINTS, LANES)


def column(scratch, k, width=HALF):
    return scratch[pl.ds(k, ROWS, stride=width), :]


def two_columns(scratch, low):
    return jnp.concatenate([column(scratch, low), column(scratch, low + LOW)], axis=0)


def keep_rows(mask, starts_ref, row_at, col_at):
    wide = jnp.concatenate([mask, mask], axis=1)
    shape = (COLS, LANES)
    lane = lax.broadcasted_iota(jnp.int32, shape, 1)
    row_ids = row_at * ROWS + jnp.where(lane < ROWS, lane, lane - ROWS)
    col_ids = col_at * COLS + lax.broadcasted_iota(jnp.int32, shape, 0)
    row_chain = jnp.zeros(shape, jnp.int32)
    col_chain = jnp.zeros(shape, jnp.int32)
    for at in range(starts_ref.shape[0]):
        start_at = starts_ref[at]
        row_chain = row_chain + (row_ids >= start_at).astype(jnp.int32)
        col_chain = col_chain + (col_ids >= start_at).astype(jnp.int32)
    return jnp.where((row_chain == col_chain) | (wide > 0), 1.0, 0.0)


def halves(a, b):
    return jnp.where(lax.broadcasted_iota(jnp.int32, a.shape, 1) < ROWS, a, b)


def edges_kernel(
    starts_ref, act_ref, mask_ref, gain_ref, bias_ref, w_ref, edges_ref, keep_ref,
    tile, kept, x_all, projected, turned,
):
    slab_at = lax.axis_index("slab")
    row_at = lax.axis_index("x") * 2 + lax.axis_index("core")
    col_at = lax.axis_index("y") * 4 + lax.axis_index("z")
    kept[...] = keep_rows(mask_ref[...], starts_ref, row_at, col_at)
    start = pl.multiple_of(slab_at * HALF, HALF)
    keep_ref[...] = halves(kept[pl.ds(start, LOW), :], kept[pl.ds(start + LOW, LOW), :])
    own = []
    for at in range(2):
        first, second = mix(w_ref[:, block(at)].astype(F32), w_ref[:, block(at + 2)].astype(F32))
        own.append(jnp.where(slab_at == 0, first, second).astype(BF16))
    w_own = jnp.concatenate(own, axis=1)
    values = act_ref[...].astype(F32)
    spare = jnp.zeros((ROWS, PITCH - COLS, LANES), F32)
    tile[...] = jnp.concatenate([values, spare], axis=1).reshape(ROWS * PITCH, LANES)
    gain, bias = (jnp.broadcast_to(ref[...], (LANES, LANES)).T for ref in (gain_ref, bias_ref))
    for k in range(HALF):
        values = jnp.concatenate([column(tile, k, PITCH), column(tile, k + HALF, PITCH)], axis=0)
        normed, _ = normalize(values.T)
        x_all[:, block(k)] = (normed * gain + bias).astype(BF16)
        if k % 4 == 3:
            here = slice((k - 3) * LANES, (k + 1) * LANES)
            projected[:, here] = dot(w_own, x_all[:, here], 0, 0)
    for k in range(HALF):
        both = jax.nn.sigmoid(projected[0:128, block(k)]) * projected[128:256, block(k)]
        both = both * halves(kept[k : k + 1, :], kept[k + HALF : k + HALF + 1, :])
        turned[pl.ds(k, OWN, stride=PITCH), :] = both[0:OWN, :]
        turned[pl.ds(k + HALF, OWN, stride=PITCH), :] = both[OWN:CHANNELS, :]
    done = turned[...].reshape(OWN, PITCH, LANES)[:, 0:COLS, :]
    edges_ref[...] = done.reshape(OWN * COLS, LANES).astype(BF16)


def ahead_kernel(
    act_ref, grad_ref, keep_ref, w_proj_ref, w_gate_ref, w_out_ref, gain_ref, bias_ref, in_gain_ref, in_bias_ref,
    slope_ref, grad_hat_ref, factor_ref, normed_ref, inv_ref, tall_ref, tile, x_in, projected,
):
    for at, ref in enumerate((in_gain_ref, gain_ref, bias_ref)):
        tall_ref[at] = jnp.broadcast_to(ref[...], (LANES, LANES)).T
    slab_at = lax.axis_index("slab")
    in_bias = jnp.broadcast_to(in_bias_ref[...], (LANES, LANES)).T
    load_half(act_ref, slab_at, tile)
    for low in range(LOW):
        normed, inv = normalize(two_columns(tile, low).T)
        normed_ref[:, block(low)] = normed
        inv_ref[:, block(low)] = inv
        x_in[:, block(low)] = (normed * tall_ref[0] + in_bias).astype(BF16)
    load_half(grad_ref, slab_at, tile)
    gain = tall_ref[1]
    for low in range(LOW):
        here = pl.ds(low * LANES, LANES)
        gate = jax.nn.sigmoid(dot(x_in[:, block(low)], w_gate_ref[...], 0, 0))
        grad_in = two_columns(tile, low)
        slope_ref[here, :] = grad_in * gate * (1.0 - gate)
        mid_in_grad = (grad_in * gate).astype(BF16)
        grad_hat = dot(w_out_ref[...], mid_in_grad, 1, 1) * gain
        grad_hat_ref[pl.ds(low, CHANNELS, stride=LOW), :] = grad_hat - jnp.mean(grad_hat, axis=0, keepdims=True)
    projected[...] = dot(w_proj_ref[...], x_in[...], 0, 0)
    for low in range(LOW):
        keep = keep_ref[low : low + 1, :]
        for side in range(2):
            at = side * 256
            sig = jax.nn.sigmoid(projected[at : at + 128, block(low)])
            value = projected[at + 128 : at + 256, block(low)]
            factor_ref[at : at + 128, block(low)] = (keep * value * sig * (1.0 - sig)).astype(BF16)
            factor_ref[at + 128 : at + 256, block(low)] = (keep * sig).astype(BF16)


def sort(edges_ref, side, ref):
    for m in range(LINES // 2):
        a, b = (
            jnp.concatenate(
                [
                    edges_ref[pl.ds((z * 16 + x * 4 + y) * COLS + side * HALF, HALF), :].astype(F32)
                    for z in range(LINES)
                    for y in range(LINES)
                ],
                axis=0,
            )
            for x in (2 * m, 2 * m + 1)
        )
        first, second = mix(a, b)
        both = jnp.concatenate(
            [first.reshape(16, HALF, LANES), second.reshape(16, HALF, LANES)], axis=1
        )
        ref[:, block(m)] = both.reshape(512, LANES).astype(BF16)


def sort_kernel(edges_ref, right_ref):
    sort(edges_ref, 1, right_ref)


def pieces_of(left_ref, right_ref, put):
    both = dot(right_ref[...], left_ref[...], 0, 0)
    for m in range(LINES // 2):
        tri = both[:, block(m)].reshape(16, HALF, LANES)
        a = tri[:, 0:LOW, :].reshape(LANES, LANES)
        b = tri[:, LOW:HALF, :].reshape(LANES, LANES)
        for x, part in zip((2 * m, 2 * m + 1), mix(a, b)):
            part = part.reshape(LINES, 2, HALF, LANES)
            for z in range(2):
                put((z * 4 + x) * 64, part[:, z].reshape(64, LANES).astype(BF16))


def own_kernel(edges_ref, own_ref, left_ref, out_ref):
    sort(edges_ref, 0, left_ref)

    def put(at, rows):
        out_ref[pl.ds(at, 64), :] = rows

    pieces_of(left_ref, own_ref, put)


def other_kernel(left_ref, other_ref, part_ref, out_ref):
    core_at = lax.axis_index("core")
    out_ref[pl.ds(pl.multiple_of(core_at * 512, 512), 512), :] = part_ref[...]
    start = (1 - core_at) * 512

    def put(at, rows):
        out_ref[pl.ds(pl.multiple_of(start + at, 64), 64), :] = rows

    pieces_of(left_ref, other_ref, put)


def middle_kernel(tri_ref, grad_hat_ref, out_ref, hats_ref):
    parts = tri_ref[...].astype(F32).reshape(OWN, 2 * LOW, LANES)
    tri = jnp.concatenate([parts[:, 0:LOW, :], parts[:, LOW : 2 * LOW, :]], axis=0)
    average = jnp.mean(tri, axis=0, keepdims=True)
    centred = tri - average
    inv = lax.rsqrt(jnp.mean(centred * centred, axis=0, keepdims=True) + 1e-05)
    hat = centred * inv
    hats_ref[...] = hat.reshape(CHANNELS * LOW, LANES)
    grad_hat = grad_hat_ref[...].reshape(CHANNELS, LOW, LANES)
    second = jnp.mean(grad_hat * hat, axis=0, keepdims=True)
    done = (grad_hat - hat * second) * inv
    both = jnp.concatenate([done[0:OWN], done[OWN:CHANNELS]], axis=1)
    out_ref[...] = both.astype(BF16).reshape(CHANNELS * LOW, LANES)


def two_rows(grad):
    grad = grad.reshape(32, HALF, LANES)
    return mix(grad[:, 0:LOW, :].reshape(256, LANES), grad[:, LOW:HALF, :].reshape(256, LANES))


def late_kernel(
    hats_ref, slope_ref, w_gate_ref, w_out_ref, tall_ref, left_ref, own_ref, other_ref, grid_t_ref,
    out_ref, left_grad_ref, right_grad_ref,
):
    right_grad_ref[...] = dot(left_ref[...], grid_t_ref[0], 1, 1)
    left_grad = dot(own_ref[...], grid_t_ref[0], 1, 0) + dot(other_ref[...], grid_t_ref[1], 1, 0)
    for m in range(LINES // 2):
        left_grad_ref[2 * m], left_grad_ref[2 * m + 1] = two_rows(left_grad[:, block(m)])
    gain, bias = tall_ref[1], tall_ref[2]
    for low in range(0, LOW, 2):
        hats = [hats_ref[pl.ds(low + at, CHANNELS, stride=LOW), :] for at in range(2)]
        mid_out = jnp.concatenate([(hat * gain + bias).astype(BF16) for hat in hats], axis=1)
        proj_out = dot(mid_out, w_out_ref[...], 0, 0)
        gate_grad = (slope_ref[pl.ds(low * LANES, 2 * LANES), :] * proj_out).astype(BF16)
        out_ref[:, low * LANES : (low + 2) * LANES] = dot(w_gate_ref[...], gate_grad, 1, 1)


def grads_kernel(tri_grad_ref, left_ref, other_ref, grid_t):
    core_at = lax.axis_index("core")
    for group, core in enumerate((core_at, 1 - core_at)):
        for m in range(LINES // 2):
            a, b = (
                jnp.concatenate(
                    [
                        tri_grad_ref[
                            pl.ds(pl.multiple_of(core * 512 + (z * 16 + x * 4 + y) * HALF, HALF), HALF), :
                        ].astype(F32)
                        for y in range(LINES)
                        for z in range(2)
                    ],
                    axis=0,
                )
                for x in (2 * m, 2 * m + 1)
            )
            first, second = mix(a, b)
            both = jnp.concatenate(
                [first.reshape(16, LOW, LANES), second.reshape(16, LOW, LANES)], axis=1
            )
            grid_t[group, :, block(m)] = both.reshape(256, LANES).astype(BF16)
    other_ref[...] = dot(left_ref[...], grid_t[1], 1, 1).astype(BF16)


def join_kernel(left_grad_ref, own_ref, other_ref, out_ref):
    for m in range(LINES // 2):
        right_grad = own_ref[:, block(m)] + other_ref[:, block(m)].astype(F32)
        for x, part in zip((2 * m, 2 * m + 1), two_rows(right_grad)):
            left_grad = left_grad_ref[x].reshape(32, LOW, LANES)
            both = jnp.concatenate([left_grad, part.reshape(32, LOW, LANES)], axis=1)
            both = both.astype(BF16).reshape(512, LANES)
            for z in range(LINES):
                out_ref[pl.ds((z * 4 + x) * LANES, LANES), :] = both[z * LANES : (z + 1) * LANES]


def final_kernel(
    grads_ref, factor_ref, part_ref, normed_ref, inv_ref, w_proj_ref, tall_ref, out_ref,
    grads, proj_grad, result,
):
    got = grads_ref[...].astype(F32).reshape(OWN, 2, HALF, LANES)
    spare = jnp.zeros((OWN, STEP - HALF, LANES), F32)
    for slab in range(2):
        part = jnp.concatenate([got[:, slab], spare], axis=1)
        grads[pl.ds(slab * OWN * STEP, OWN * STEP), :] = part.reshape(OWN * STEP, LANES)

    def fill(low):
        for side in range(2):
            grad = jnp.concatenate(
                [
                    grads[pl.ds(slab * OWN * STEP + side * LOW + low, OWN, stride=STEP), :]
                    for slab in range(2)
                ],
                axis=0,
            )
            for at in (side * 256, side * 256 + 128):
                factor = factor_ref[at : at + 128, block(low)].astype(F32)
                proj_grad[at : at + 128, block(low)] = (grad * factor).astype(BF16)

    gain = tall_ref[0]
    for low in range(0, LOW, 2):
        fill(low)
        fill(low + 1)
        pair = dot(w_proj_ref[...], proj_grad[:, low * LANES : (low + 2) * LANES], 1, 0)
        for at in range(2):
            x_grad = pair[:, block(at)] + part_ref[:, block(low + at)]
            normed = normed_ref[:, block(low + at)]
            in_hat = x_grad * gain
            first = jnp.mean(in_hat, axis=0, keepdims=True)
            second = jnp.mean(in_hat * normed, axis=0, keepdims=True)
            done = ((in_hat - first - normed * second) * inv_ref[:, block(low + at)]).T
            result[pl.ds(low + at, ROWS, stride=STEP), :] = done[0:ROWS, :]
            result[pl.ds(low + at + LOW, ROWS, stride=STEP), :] = done[ROWS:LANES, :]
    out_ref[...] = result[...].reshape(ROWS, STEP, LANES)[:, 0:HALF, :].astype(BF16)


SMEM = pl.BlockSpec(memory_space=pltpu.SMEM)
VMEM = pl.BlockSpec(memory_space=pltpu.VMEM)


def call(kernel, outs, scratch, args, name, smem=0, cost=None, room=24):
    single = not isinstance(outs, list)
    return pl.pallas_call(
        kernel,
        out_shape=outs,
        in_specs=[SMEM] * smem + [VMEM] * (len(args) - smem),
        out_specs=VMEM if single else [VMEM] * len(outs),
        scratch_shapes=scratch,
        compiler_params=pltpu.CompilerParams(vmem_limit_bytes=room * 1024 * 1024),
        cost_estimate=cost,
        name=name,
    )(*args)


def shape(dims, kind):
    return jax.ShapeDtypeStruct(dims, kind)


def exchange(flat, axes):
    pieces = lax.axis_size(axes)
    cut = flat.reshape(pieces, flat.shape[0] // pieces, LANES)
    return lax.all_to_all(cut, axes, 0, 0, tiled=True).reshape(flat.shape)


def swap(x):
    return lax.ppermute(x, "core", [(0, 1), (1, 0)])


def on_device(
    pair_act, out_grad, pair_mask, chain_starts, in_gain, in_bias, w_proj, w_gate, w_out, mid_gain, mid_bias
):
    in_gain, in_bias, mid_gain, mid_bias = (
        v.reshape(1, LANES) for v in (in_gain, in_bias, mid_gain, mid_bias)
    )
    edge_rows = OWN * COLS
    tri_rows = CHANNELS * LOW
    edges, keep = call(
        edges_kernel,
        [shape((edge_rows, LANES), BF16), shape((LOW, LANES), F32)],
        [
            pltpu.VMEM((ROWS * PITCH, LANES), F32),
            pltpu.VMEM((COLS, LANES), F32),
            pltpu.VMEM((LANES, 2 * POINTS), BF16),
            pltpu.VMEM((256, 2 * POINTS), F32),
            pltpu.VMEM((OWN * PITCH, LANES), F32),
        ],
        (chain_starts, pair_act, pair_mask.T, in_gain, in_bias, w_proj),
        "edges",
        smem=1,
        room=63,
    )
    edges = exchange(edges, NEAR)
    slope, grad_hat, factor, normed, inv, tall = call(
        ahead_kernel,
        [
            shape((POINTS, LANES), F32),
            shape((tri_rows, LANES), F32),
            shape((512, POINTS), BF16),
            shape((LANES, POINTS), F32),
            shape((1, POINTS), F32),
            shape((3, LANES, LANES), F32),
        ],
        [
            pltpu.VMEM((POINTS, LANES), F32),
            pltpu.VMEM((LANES, POINTS), BF16),
            pltpu.VMEM((512, POINTS), F32),
        ],
        (pair_act, out_grad, keep, w_proj, w_gate, w_out, mid_gain, mid_bias, in_gain, in_bias),
        "ahead",
        cost=pl.CostEstimate(flops=300_000_000, bytes_accessed=6_000_000, transcendentals=700_000),
    )
    edges, slope, grad_hat, factor, normed, inv, tall = lax.optimization_barrier(
        (edges, slope, grad_hat, factor, normed, inv, tall)
    )
    own = call(sort_kernel, shape((512, 256), BF16), [], (edges,), "sort")
    other = swap(own)
    left, part = call(
        own_kernel,
        [shape((512, 256), BF16), shape((tri_rows // 2, LANES), BF16)],
        [],
        (edges, own),
        "triangle_own",
    )
    other, left, part = lax.optimization_barrier((other, left, part))
    tri = call(
        other_kernel, shape((tri_rows, LANES), BF16), [], (left, other, part), "triangle_other"
    )
    tri = exchange(tri, FAR)
    tri_grad, hats = call(
        middle_kernel,
        [shape((tri_rows, LANES), BF16), shape((tri_rows, LANES), F32)],
        [],
        (tri, grad_hat),
        "middle",
    )
    tri_grad = exchange(tri_grad, FAR)
    other_grad, grid_t = call(
        grads_kernel,
        [shape((512, 256), BF16), shape((2, 256, 256), BF16)],
        [],
        (tri_grad, left),
        "grads",
    )
    other_grad, hats, grid_t = lax.optimization_barrier((other_grad, hats, grid_t))
    swapped = swap(other_grad)
    part, left_grad, own_grad = call(
        late_kernel,
        [shape((LANES, POINTS), F32), shape((LINES, 256, LANES), F32), shape((512, 256), F32)],
        [],
        (hats, slope, w_gate, w_out, tall, left, own, other, grid_t),
        "late",
        cost=pl.CostEstimate(flops=210_000_000, bytes_accessed=3_000_000, transcendentals=0),
    )
    swapped, part, left_grad, own_grad = lax.optimization_barrier((swapped, part, left_grad, own_grad))
    grads = call(
        join_kernel, shape((CHANNELS * HALF, LANES), BF16), [], (left_grad, own_grad, swapped), "join"
    )
    grads = exchange(grads, FAR)
    result = call(
        final_kernel,
        shape((ROWS, HALF, LANES), BF16),
        [
            pltpu.VMEM((CHANNELS * STEP, LANES), F32),
            pltpu.VMEM((512, POINTS), BF16),
            pltpu.VMEM((ROWS * STEP, LANES), F32),
        ],
        (grads, factor, part, normed, inv, w_proj, tall),
        "final",
    )
    return result.reshape(ROWS, 1, 1, HALF, LANES)


def solution(mesh):
    fine = Mesh(mesh.devices.reshape(2, LINES, 2, 4, 4), ("slab", "x", "core", "y", "z"))
    row, col = ("x", "core"), ("y", "z")
    in_specs = (P(row, col, None), P(row, col, None), P(row, col)) + (P(),) * 8
    out_specs = P(row, col, "slab", None, None)
    return jax.shard_map(
        on_device, mesh=fine, in_specs=in_specs, out_specs=out_specs, check_vma=False
    )
```

```python
import jax
import jax.numpy as jnp
from jax import lax
from jax.experimental import pallas as pl
from jax.experimental.pallas import tpu as pltpu
from jax.sharding import Mesh
from jax.sharding import PartitionSpec as P

BF16 = jnp.bfloat16
F32 = jnp.float32
LANES = 128
ROWS = 64
HALF = 16
COLS = 2 * HALF
LOW = 8
CHANNELS = 128
OWN = CHANNELS // 2
POINTS = ROWS * HALF
PITCH = COLS + 8
STEP = HALF + 8
LINES = 4
NEAR = ("z", "x", "y")
FAR = ("z", "x", "y", "slab")


def dot(a, b, ca, cb):
    return lax.dot_general(a, b, (((ca,), (cb,)), ((), ())), preferred_element_type=F32)


def normalize(values):
    average = jnp.mean(values, axis=0, keepdims=True)
    centred = values - average
    inv_std = lax.rsqrt(jnp.mean(centred * centred, axis=0, keepdims=True) + 1e-05)
    return centred * inv_std, inv_std


def mix(a, b):
    low = lax.broadcasted_iota(jnp.int32, a.shape, 1) < ROWS
    first = jnp.where(low, a, pltpu.roll(b, ROWS, 1))
    second = jnp.where(low, pltpu.roll(a, ROWS, 1), b)
    return first, second


def block(m):
    return slice(m * LANES, (m + 1) * LANES)


def load_half(ref, slab_at, scratch):
    start = pl.multiple_of(slab_at * HALF, HALF)
    scratch[...] = ref[:, pl.ds(start, HALF), :].astype(F32).reshape(POINTS, LANES)


def column(scratch, k, width=HALF):
    return scratch[pl.ds(k, ROWS, stride=width), :]


def two_columns(scratch, low):
    return jnp.concatenate([column(scratch, low), column(scratch, low + LOW)], axis=0)


def keep_rows(mask, starts_ref, row_at, col_at):
    wide = jnp.concatenate([mask, mask], axis=1)
    shape = (COLS, LANES)
    lane = lax.broadcasted_iota(jnp.int32, shape, 1)
    row_ids = row_at * ROWS + jnp.where(lane < ROWS, lane, lane - ROWS)
    col_ids = col_at * COLS + lax.broadcasted_iota(jnp.int32, shape, 0)
    row_chain = jnp.zeros(shape, jnp.int32)
    col_chain = jnp.zeros(shape, jnp.int32)
    for at in range(starts_ref.shape[0]):
        start_at = starts_ref[at]
        row_chain = row_chain + (row_ids >= start_at).astype(jnp.int32)
        col_chain = col_chain + (col_ids >= start_at).astype(jnp.int32)
    return jnp.where((row_chain == col_chain) | (wide > 0), 1.0, 0.0)


def halves(a, b):
    return jnp.where(lax.broadcasted_iota(jnp.int32, a.shape, 1) < ROWS, a, b)


def edges_kernel(
    starts_ref, act_ref, mask_ref, gain_ref, bias_ref, w_ref, edges_ref, keep_ref,
    tile, kept, x_all, projected, turned,
):
    slab_at = lax.axis_index("slab")
    row_at = lax.axis_index("x") * 2 + lax.axis_index("core")
    col_at = lax.axis_index("y") * 4 + lax.axis_index("z")
    kept[...] = keep_rows(mask_ref[...], starts_ref, row_at, col_at)
    start = pl.multiple_of(slab_at * HALF, HALF)
    keep_ref[...] = halves(kept[pl.ds(start, LOW), :], kept[pl.ds(start + LOW, LOW), :])
    own = []
    for at in range(2):
        first, second = mix(w_ref[:, block(at)].astype(F32), w_ref[:, block(at + 2)].astype(F32))
        own.append(jnp.where(slab_at == 0, first, second).astype(BF16))
    w_own = jnp.concatenate(own, axis=1)
    values = act_ref[...].astype(F32)
    spare = jnp.zeros((ROWS, PITCH - COLS, LANES), F32)
    tile[...] = jnp.concatenate([values, spare], axis=1).reshape(ROWS * PITCH, LANES)
    gain, bias = (jnp.broadcast_to(ref[...], (LANES, LANES)).T for ref in (gain_ref, bias_ref))
    for k in range(HALF):
        values = jnp.concatenate([column(tile, k, PITCH), column(tile, k + HALF, PITCH)], axis=0)
        normed, _ = normalize(values.T)
        x_all[:, block(k)] = (normed * gain + bias).astype(BF16)
        if k % 4 == 3:
            here = slice((k - 3) * LANES, (k + 1) * LANES)
            projected[:, here] = dot(w_own, x_all[:, here], 0, 0)
    for k in range(HALF):
        both = jax.nn.sigmoid(projected[0:128, block(k)]) * projected[128:256, block(k)]
        both = both * halves(kept[k : k + 1, :], kept[k + HALF : k + HALF + 1, :])
        turned[pl.ds(k, OWN, stride=PITCH), :] = both[0:OWN, :]
        turned[pl.ds(k + HALF, OWN, stride=PITCH), :] = both[OWN:CHANNELS, :]
    done = turned[...].reshape(OWN, PITCH, LANES)[:, 0:COLS, :]
    edges_ref[...] = done.reshape(OWN * COLS, LANES).astype(BF16)


def ahead_kernel(
    act_ref, grad_ref, keep_ref, w_proj_ref, w_gate_ref, w_out_ref, gain_ref, bias_ref, in_gain_ref, in_bias_ref,
    slope_ref, grad_hat_ref, factor_ref, normed_ref, inv_ref, tall_ref, tile, x_in, projected,
):
    for at, ref in enumerate((in_gain_ref, gain_ref, bias_ref)):
        tall_ref[at] = jnp.broadcast_to(ref[...], (LANES, LANES)).T
    slab_at = lax.axis_index("slab")
    in_bias = jnp.broadcast_to(in_bias_ref[...], (LANES, LANES)).T
    load_half(act_ref, slab_at, tile)
    for low in range(LOW):
        normed, inv = normalize(two_columns(tile, low).T)
        normed_ref[:, block(low)] = normed
        inv_ref[:, block(low)] = inv
        x_in[:, block(low)] = (normed * tall_ref[0] + in_bias).astype(BF16)
    load_half(grad_ref, slab_at, tile)
    gain = tall_ref[1]
    for low in range(LOW):
        here = pl.ds(low * LANES, LANES)
        gate = jax.nn.sigmoid(dot(x_in[:, block(low)], w_gate_ref[...], 0, 0))
        grad_in = two_columns(tile, low)
        slope_ref[here, :] = grad_in * gate * (1.0 - gate)
        mid_in_grad = (grad_in * gate).astype(BF16)
        grad_hat = dot(w_out_ref[...], mid_in_grad, 1, 1) * gain
        grad_hat_ref[pl.ds(low, CHANNELS, stride=LOW), :] = grad_hat - jnp.mean(grad_hat, axis=0, keepdims=True)
    projected[...] = dot(w_proj_ref[...], x_in[...], 0, 0)
    for low in range(LOW):
        keep = keep_ref[low : low + 1, :]
        for side in range(2):
            at = side * 256
            sig = jax.nn.sigmoid(projected[at : at + 128, block(low)])
            value = projected[at + 128 : at + 256, block(low)]
            factor_ref[at : at + 128, block(low)] = (keep * value * sig * (1.0 - sig)).astype(BF16)
            factor_ref[at + 128 : at + 256, block(low)] = (keep * sig).astype(BF16)


def sort(edges_ref, side, ref):
    for m in range(LINES // 2):
        a, b = (
            jnp.concatenate(
                [
                    edges_ref[pl.ds((z * 16 + x * 4 + y) * COLS + side * HALF, HALF), :].astype(F32)
                    for z in range(LINES)
                    for y in range(LINES)
                ],
                axis=0,
            )
            for x in (2 * m, 2 * m + 1)
        )
        first, second = mix(a, b)
        both = jnp.concatenate(
            [first.reshape(16, HALF, LANES), second.reshape(16, HALF, LANES)], axis=1
        )
        ref[:, block(m)] = both.reshape(512, LANES).astype(BF16)


def sort_kernel(edges_ref, right_ref):
    sort(edges_ref, 1, right_ref)


def pieces_of(left_ref, right_ref, put):
    both = dot(right_ref[...], left_ref[...], 0, 0)
    for m in range(LINES // 2):
        tri = both[:, block(m)].reshape(16, HALF, LANES)
        a = tri[:, 0:LOW, :].reshape(LANES, LANES)
        b = tri[:, LOW:HALF, :].reshape(LANES, LANES)
        for x, part in zip((2 * m, 2 * m + 1), mix(a, b)):
            part = part.reshape(LINES, 2, HALF, LANES)
            for z in range(2):
                put((z * 4 + x) * 64, part[:, z].reshape(64, LANES).astype(BF16))


def own_kernel(edges_ref, own_ref, left_ref, out_ref):
    sort(edges_ref, 0, left_ref)

    def put(at, rows):
        out_ref[pl.ds(at, 64), :] = rows

    pieces_of(left_ref, own_ref, put)


def other_kernel(left_ref, other_ref, part_ref, out_ref):
    core_at = lax.axis_index("core")
    out_ref[pl.ds(pl.multiple_of(core_at * 512, 512), 512), :] = part_ref[...]
    start = (1 - core_at) * 512

    def put(at, rows):
        out_ref[pl.ds(pl.multiple_of(start + at, 64), 64), :] = rows

    pieces_of(left_ref, other_ref, put)


def tri_norm(tri_ref):
    parts = tri_ref[...].astype(F32).reshape(OWN, 2 * LOW, LANES)
    return normalize(jnp.concatenate([parts[:, 0:LOW, :], parts[:, LOW : 2 * LOW, :]], axis=0))


def middle_kernel(tri_ref, grad_hat_ref, out_ref):
    hat, inv = tri_norm(tri_ref)
    grad_hat = grad_hat_ref[...].reshape(CHANNELS, LOW, LANES)
    second = jnp.mean(grad_hat * hat, axis=0, keepdims=True)
    done = (grad_hat - hat * second) * inv
    both = jnp.concatenate([done[0:OWN], done[OWN:CHANNELS]], axis=1)
    out_ref[...] = both.astype(BF16).reshape(CHANNELS * LOW, LANES)


def two_rows(grad):
    grad = grad.reshape(32, HALF, LANES)
    return mix(grad[:, 0:LOW, :].reshape(256, LANES), grad[:, LOW:HALF, :].reshape(256, LANES))


def late_kernel(
    tri_ref, slope_ref, w_gate_ref, w_out_ref, tall_ref, left_ref, own_ref, other_ref, grid_t_ref,
    out_ref, left_grad_ref, right_grad_ref, hats_ref,
):
    hats_ref[...] = tri_norm(tri_ref)[0].reshape(CHANNELS * LOW, LANES)
    right_grad_ref[...] = dot(left_ref[...], grid_t_ref[0], 1, 1)
    left_grad = dot(own_ref[...], grid_t_ref[0], 1, 0) + dot(other_ref[...], grid_t_ref[1], 1, 0)
    for m in range(LINES // 2):
        left_grad_ref[2 * m], left_grad_ref[2 * m + 1] = two_rows(left_grad[:, block(m)])
    gain, bias = tall_ref[1], tall_ref[2]
    for low in range(0, LOW, 2):
        hats = [hats_ref[pl.ds(low + at, CHANNELS, stride=LOW), :] for at in range(2)]
        mid_out = jnp.concatenate([(hat * gain + bias).astype(BF16) for hat in hats], axis=1)
        proj_out = dot(mid_out, w_out_ref[...], 0, 0)
        gate_grad = (slope_ref[pl.ds(low * LANES, 2 * LANES), :] * proj_out).astype(BF16)
        out_ref[:, low * LANES : (low + 2) * LANES] = dot(w_gate_ref[...], gate_grad, 1, 1)


def grads_kernel(tri_grad_ref, left_ref, other_ref, grid_t):
    core_at = lax.axis_index("core")
    for group, core in enumerate((core_at, 1 - core_at)):
        for m in range(LINES // 2):
            a, b = (
                jnp.concatenate(
                    [
                        tri_grad_ref[
                            pl.ds(pl.multiple_of(core * 512 + (z * 16 + x * 4 + y) * HALF, HALF), HALF), :
                        ].astype(F32)
                        for y in range(LINES)
                        for z in range(2)
                    ],
                    axis=0,
                )
                for x in (2 * m, 2 * m + 1)
            )
            first, second = mix(a, b)
            both = jnp.concatenate(
                [first.reshape(16, LOW, LANES), second.reshape(16, LOW, LANES)], axis=1
            )
            grid_t[group, :, block(m)] = both.reshape(256, LANES).astype(BF16)
    other_ref[...] = dot(left_ref[...], grid_t[1], 1, 1).astype(BF16)


def join_kernel(left_grad_ref, own_ref, other_ref, out_ref):
    for m in range(LINES // 2):
        right_grad = own_ref[:, block(m)] + other_ref[:, block(m)].astype(F32)
        for x, part in zip((2 * m, 2 * m + 1), two_rows(right_grad)):
            left_grad = left_grad_ref[x].reshape(32, LOW, LANES)
            both = jnp.concatenate([left_grad, part.reshape(32, LOW, LANES)], axis=1)
            both = both.astype(BF16).reshape(512, LANES)
            for z in range(LINES):
                out_ref[pl.ds((z * 4 + x) * LANES, LANES), :] = both[z * LANES : (z + 1) * LANES]


def final_kernel(
    grads_ref, factor_ref, part_ref, normed_ref, inv_ref, w_proj_ref, tall_ref, out_ref,
    grads, proj_grad, result,
):
    got = grads_ref[...].astype(F32).reshape(OWN, 2, HALF, LANES)
    spare = jnp.zeros((OWN, STEP - HALF, LANES), F32)
    for slab in range(2):
        part = jnp.concatenate([got[:, slab], spare], axis=1)
        grads[pl.ds(slab * OWN * STEP, OWN * STEP), :] = part.reshape(OWN * STEP, LANES)

    def fill(low):
        for side in range(2):
            grad = jnp.concatenate(
                [
                    grads[pl.ds(slab * OWN * STEP + side * LOW + low, OWN, stride=STEP), :]
                    for slab in range(2)
                ],
                axis=0,
            )
            for at in (side * 256, side * 256 + 128):
                factor = factor_ref[at : at + 128, block(low)].astype(F32)
                proj_grad[at : at + 128, block(low)] = (grad * factor).astype(BF16)

    gain = tall_ref[0]
    for low in range(0, LOW, 2):
        fill(low)
        fill(low + 1)
        pair = dot(w_proj_ref[...], proj_grad[:, low * LANES : (low + 2) * LANES], 1, 0)
        for at in range(2):
            x_grad = pair[:, block(at)] + part_ref[:, block(low + at)]
            normed = normed_ref[:, block(low + at)]
            in_hat = x_grad * gain
            first = jnp.mean(in_hat, axis=0, keepdims=True)
            second = jnp.mean(in_hat * normed, axis=0, keepdims=True)
            done = ((in_hat - first - normed * second) * inv_ref[:, block(low + at)]).T
            result[pl.ds(low + at, ROWS, stride=STEP), :] = done[0:ROWS, :]
            result[pl.ds(low + at + LOW, ROWS, stride=STEP), :] = done[ROWS:LANES, :]
    out_ref[...] = result[...].reshape(ROWS, STEP, LANES)[:, 0:HALF, :].astype(BF16)


SMEM = pl.BlockSpec(memory_space=pltpu.SMEM)
VMEM = pl.BlockSpec(memory_space=pltpu.VMEM)


def call(kernel, outs, scratch, args, name, smem=0, cost=None, room=24):
    single = not isinstance(outs, list)
    return pl.pallas_call(
        kernel,
        out_shape=outs,
        in_specs=[SMEM] * smem + [VMEM] * (len(args) - smem),
        out_specs=VMEM if single else [VMEM] * len(outs),
        scratch_shapes=scratch,
        compiler_params=pltpu.CompilerParams(vmem_limit_bytes=room * 1024 * 1024),
        cost_estimate=cost,
        name=name,
    )(*args)


def shape(dims, kind):
    return jax.ShapeDtypeStruct(dims, kind)


def exchange(flat, axes):
    pieces = lax.axis_size(axes)
    cut = flat.reshape(pieces, flat.shape[0] // pieces, LANES)
    return lax.all_to_all(cut, axes, 0, 0, tiled=True).reshape(flat.shape)


def swap(x):
    return lax.ppermute(x, "core", [(0, 1), (1, 0)])


def on_device(
    pair_act, out_grad, pair_mask, chain_starts, in_gain, in_bias, w_proj, w_gate, w_out, mid_gain, mid_bias
):
    in_gain, in_bias, mid_gain, mid_bias = (
        v.reshape(1, LANES) for v in (in_gain, in_bias, mid_gain, mid_bias)
    )
    edge_rows = OWN * COLS
    tri_rows = CHANNELS * LOW
    edges, keep = call(
        edges_kernel,
        [shape((edge_rows, LANES), BF16), shape((LOW, LANES), F32)],
        [
            pltpu.VMEM((ROWS * PITCH, LANES), F32),
            pltpu.VMEM((COLS, LANES), F32),
            pltpu.VMEM((LANES, 2 * POINTS), BF16),
            pltpu.VMEM((256, 2 * POINTS), F32),
            pltpu.VMEM((OWN * PITCH, LANES), F32),
        ],
        (chain_starts, pair_act, pair_mask.T, in_gain, in_bias, w_proj),
        "edges",
        smem=1,
        room=63,
    )
    edges = exchange(edges, NEAR)
    slope, grad_hat, factor, normed, inv, tall = call(
        ahead_kernel,
        [
            shape((POINTS, LANES), F32),
            shape((tri_rows, LANES), F32),
            shape((512, POINTS), BF16),
            shape((LANES, POINTS), F32),
            shape((1, POINTS), F32),
            shape((3, LANES, LANES), F32),
        ],
        [
            pltpu.VMEM((POINTS, LANES), F32),
            pltpu.VMEM((LANES, POINTS), BF16),
            pltpu.VMEM((512, POINTS), F32),
        ],
        (pair_act, out_grad, keep, w_proj, w_gate, w_out, mid_gain, mid_bias, in_gain, in_bias),
        "ahead",
        cost=pl.CostEstimate(flops=300_000_000, bytes_accessed=6_000_000, transcendentals=700_000),
    )
    edges, slope, grad_hat, factor, normed, inv, tall = lax.optimization_barrier(
        (edges, slope, grad_hat, factor, normed, inv, tall)
    )
    own = call(sort_kernel, shape((512, 256), BF16), [], (edges,), "sort")
    other = swap(own)
    left, part = call(
        own_kernel,
        [shape((512, 256), BF16), shape((tri_rows // 2, LANES), BF16)],
        [],
        (edges, own),
        "triangle_own",
    )
    other, left, part = lax.optimization_barrier((other, left, part))
    tri = call(
        other_kernel, shape((tri_rows, LANES), BF16), [], (left, other, part), "triangle_other"
    )
    tri = exchange(tri, FAR)
    tri_grad = call(
        middle_kernel,
        shape((tri_rows, LANES), BF16),
        [],
        (tri, grad_hat),
        "middle",
    )
    tri_grad = exchange(tri_grad, FAR)
    other_grad, grid_t = call(
        grads_kernel,
        [shape((512, 256), BF16), shape((2, 256, 256), BF16)],
        [],
        (tri_grad, left),
        "grads",
    )
    other_grad, tri, grid_t = lax.optimization_barrier((other_grad, tri, grid_t))
    swapped = swap(other_grad)
    part, left_grad, own_grad = call(
        late_kernel,
        [shape((LANES, POINTS), F32), shape((LINES, 256, LANES), F32), shape((512, 256), F32)],
        [pltpu.VMEM((tri_rows, LANES), F32)],
        (tri, slope, w_gate, w_out, tall, left, own, other, grid_t),
        "late",
        cost=pl.CostEstimate(flops=210_000_000, bytes_accessed=3_000_000, transcendentals=0),
    )
    swapped, part, left_grad, own_grad = lax.optimization_barrier((swapped, part, left_grad, own_grad))
    grads = call(
        join_kernel, shape((CHANNELS * HALF, LANES), BF16), [], (left_grad, own_grad, swapped), "join"
    )
    grads = exchange(grads, FAR)
    result = call(
        final_kernel,
        shape((ROWS, HALF, LANES), BF16),
        [
            pltpu.VMEM((CHANNELS * STEP, LANES), F32),
            pltpu.VMEM((512, POINTS), BF16),
            pltpu.VMEM((ROWS * STEP, LANES), F32),
        ],
        (grads, factor, part, normed, inv, w_proj, tall),
        "final",
    )
    return result.reshape(ROWS, 1, 1, HALF, LANES)


def solution(mesh):
    fine = Mesh(mesh.devices.reshape(2, LINES, 2, 4, 4), ("slab", "x", "core", "y", "z"))
    row, col = ("x", "core"), ("y", "z")
    in_specs = (P(row, col, None), P(row, col, None), P(row, col)) + (P(),) * 8
    out_specs = P(row, col, "slab", None, None)
    return jax.shard_map(
        on_device, mesh=fine, in_specs=in_specs, out_specs=out_specs, check_vma=False
    )
```
